32 devices in a mesh: dp: 4 (over y, x), seq: 8 (over z, core).
Axes of the slice: x: 2, y: 2, z: 4, core: 2. Of those that a mesh axis runs over, the one named last changes fastest.
Arguments:
- tokens: int32 [4, 2048], P('dp', 'seq'), may hold values from 0 to 4
- mask_pos: int32 [4, 307], P('dp'), may hold values from 0 to 2047, as said below
- replace_ids: int32 [4, 307], P('dp'), may hold values from 0 to 5
- token_embedding_matrix: bfloat16 [6, 512], replicated, may hold values from -6 to 6
- entry_scale_vector: float32 [512], replicated, may hold values from 0.1 to 1.9
- input_projection_weight: bfloat16 [512, 1152], replicated, may hold values from -0.25 to 0.25
- increment_coefficients: bfloat16 [512, 8], replicated, may hold values from -0.25 to 0.25
- conv_w: float32 [2, 4, 640], replicated, may hold values from -3 to 3
- conv_b: float32 [2, 640], replicated, may hold values from -0.5 to 0.5
- dt_bias: float32 [2, 8], replicated, may hold values from -1 to 1
- decay_rate: float32 [2, 8], replicated, may hold values from 0 to 0.05, as said below
- gain_out: float32 [512], replicated, may hold values from 0.1 to 1.9
- w_out: bfloat16 [512, 512], replicated, may hold values from -0.25 to 0.25
- w_head: bfloat16 [512, 5], replicated, may hold values from -0.25 to 0.25
Outputs:
- layer_out: bfloat16 [4, 2048, 512], P('dp', 'seq')
- grad_w_out: float32 [512, 512], replicated
The draws below stay inside these ranges and needn't reach their ends.
Inputs may be any that keep to these rules, and one draw needn't show every extreme that they name: `mask_pos`: the 307 positions of one sequence are distinct. `decay_rate`: positive rates.
All inputs are finite; a program needn't handle non-finite values.
Results may differ from the reference program's by a relative error of at most 0.011.
Values may be sent and summed in bfloat16 or wider, within the bound.
No kernel may reach another device: no remote copies, remote signals or barrier semaphores. Data moves between devices by JAX's collectives and lax.ppermute only.
A program may use at most 256 MiB of HBM per device.

```python
import jax
import jax.numpy as jnp
from jax import lax

D = 512
HEADS = 8
HEADDIM = 64
STATE = 64
SPAN = 128
KW = 4
VOCAB = 5
IDS = 6
INNER = 512
CONVW = 640
SEQS = 4
LENGTH = 2048
MASKED = 307


def draw_mask_pos(key, part):
    subkeys = jax.random.split(key, SEQS)
    chosen = jax.vmap(lambda subkey: jax.random.permutation(subkey, LENGTH)[:MASKED])(subkeys)
    return chosen.astype(jnp.int32)


def draw_decay_rate(key, part):
    key_rank, key_slow, key_fast = jax.random.split(key, 3)
    ranking = jax.vmap(lambda subkey: jax.random.permutation(subkey, HEADS))(jax.random.split(key_rank, 2))
    slow_rate = jnp.exp(jax.random.uniform(key_slow, (2, HEADS), jnp.float32, jnp.log(0.1), jnp.log(1.5))) / LENGTH
    fast_rate = jnp.exp(jax.random.uniform(key_fast, (2, HEADS), jnp.float32, jnp.log(0.02), jnp.log(0.05)))
    quick_count = HEADS // 2
    return jnp.where(ranking < quick_count, fast_rate, slow_rate).astype(jnp.float32)


def set_ends(entries, stream_key, low, top_value):
    longest = entries.shape.index(max(entries.shape))
    spots = []
    for shift in (0, 1):
        where = [jax.random.randint(jax.random.fold_in(stream_key, axis), (), 0, length) for axis, length in enumerate(entries.shape)]
        where[longest] = (where[longest] + shift) % entries.shape[longest]
        spots.append(tuple(where))
    return entries.at[spots[0]].set(low).at[spots[1]].set(top_value)


def noise(own_key, dims, width, most, dtype=jnp.bfloat16):
    drawn = jax.random.normal(own_key, dims, jnp.float32) * width
    return jnp.minimum(jnp.maximum(drawn, -most), most).astype(dtype)


def setup_inputs(seed: int = 0) -> dict:
    key_of = jax.random.split(jax.random.key(seed), 15)
    return {
        "tokens": set_ends(jax.random.randint(key_of[0], (SEQS, LENGTH), 0, 5), jax.random.fold_in(key_of[0], 1), 0, 4).astype(jnp.int32),
        "mask_pos": draw_mask_pos(jax.random.fold_in(key_of[14], 71), 0),
        "replace_ids": set_ends(jax.random.randint(key_of[2], (SEQS, MASKED), 0, 6), jax.random.fold_in(key_of[2], 1), 0, 5).astype(jnp.int32),
        "token_embedding_matrix": noise(key_of[3], (IDS, D), 1.0, 6.0),
        "entry_scale_vector": jnp.clip(1.0 + 0.18 * jax.random.normal(key_of[4], (D,), jnp.float32), 0.1, 1.9),
        "input_projection_weight": noise(key_of[5], (D, INNER + CONVW), D ** -0.5, 0.25),
        "increment_coefficients": noise(key_of[6], (D, HEADS), D ** -0.5, 0.25),
        "conv_w": noise(key_of[7], (2, KW, CONVW), 0.5, 3.0, jnp.float32),
        "conv_b": jnp.clip(jax.random.uniform(key_of[8], (2, CONVW), jnp.float32, -0.5, 0.5), -0.5, 0.5),
        "dt_bias": jnp.clip(jax.random.uniform(key_of[9], (2, HEADS), jnp.float32, -1.0, 1.0), -1.0, 1.0),
        "decay_rate": draw_decay_rate(jax.random.fold_in(key_of[14], 71), 0),
        "gain_out": jnp.clip(1.0 + 0.18 * jax.random.normal(key_of[11], (INNER,), jnp.float32), 0.1, 1.9),
        "w_out": noise(key_of[12], (INNER, D), INNER ** -0.5, 0.25),
        "w_head": noise(key_of[13], (D, VOCAB), D ** -0.5, 0.25),
    }


EPSILON = 1e-05

def complement(entry_numbers):
    return jnp.where(entry_numbers < 4, 3 - entry_numbers, entry_numbers).astype(jnp.int32)

def row_norm(entry_numbers, gain):
    mean_sq = lax.optimization_barrier(jnp.mean(entry_numbers * entry_numbers, axis=-1, keepdims=True))
    return entry_numbers * lax.rsqrt(mean_sq + EPSILON) * gain

def silu_slope(entry_numbers):
    sigma = jax.nn.sigmoid(entry_numbers)
    return sigma * (1.0 + entry_numbers * (1.0 - sigma))

def filtered_lines(padded, weights, offset_lines):
    taps = weights.shape[0]
    length = padded.shape[0] - (taps - 1)
    conv_sum = jnp.broadcast_to(offset_lines[None, :], (length, padded.shape[1])).astype(jnp.float32)
    for offset in range(taps):
        first_row = taps - 1 - offset
        conv_sum = conv_sum + weights[offset][None, :] * padded[first_row:first_row + length].astype(jnp.float32)
    return jax.nn.silu(conv_sum).astype(jnp.bfloat16)

def scan_stream(conv_out, step_size, log_decay):
    length = conv_out.shape[0]
    blocks = length // SPAN
    conv_blocks = conv_out.reshape(blocks, SPAN, CONVW)
    step_blocks = step_size.reshape(blocks, SPAN, HEADS)
    decay_blocks = log_decay.reshape(blocks, SPAN, HEADS)
    causal = jnp.arange(SPAN)[:, None] >= jnp.arange(SPAN)[None, :]

    def advance(carry_state, block_in):
        conv_blk, step_blk, decay_blk = block_in
        x_rows = conv_blk[:, :INNER].reshape(SPAN, HEADS, HEADDIM).astype(jnp.float32)
        b_rows = conv_blk[:, INNER:INNER + STATE].astype(jnp.float32)
        c_rows = conv_blk[:, INNER + STATE:].astype(jnp.float32)
        cum_decay = jnp.cumsum(decay_blk, axis=0).T
        scores = jnp.dot(c_rows, b_rows.T, precision=lax.Precision.HIGHEST)
        spread = cum_decay[:, :, None] - cum_decay[:, None, :]
        factor = jnp.where(causal, jnp.exp(jnp.where(causal, spread, 0.0)), 0.0)
        weights = (scores[None] * factor * step_blk.T[:, None, :]).astype(jnp.bfloat16)
        intra_out = jnp.einsum('hij,jhp->ihp', weights.astype(jnp.float32), x_rows, precision=lax.Precision.HIGHEST)
        cum_rows = cum_decay.T
        carried = jnp.exp(cum_rows)[:, :, None] * jnp.einsum('in,hnp->ihp', c_rows, carry_state, precision=lax.Precision.HIGHEST)
        block_last = cum_decay[:, -1]
        scaled = (x_rows * (jnp.exp(block_last[None, :] - cum_rows) * step_blk)[:, :, None]).astype(jnp.bfloat16)
        block_state = jnp.einsum('jn,jhp->hnp', b_rows, scaled.astype(jnp.float32), precision=lax.Precision.HIGHEST)
        next_state = jnp.exp(block_last)[:, None, None] * carry_state + block_state
        return (next_state, (intra_out + carried).reshape(SPAN, INNER))
    initial = jnp.zeros((HEADS, STATE, HEADDIM), jnp.float32)
    _, outputs = lax.scan(advance, initial, (conv_blocks, step_blocks, decay_blocks))
    return outputs.reshape(length, INNER)

def reference(tokens, mask_pos, replace_ids, token_embedding_matrix, entry_scale_vector, input_projection_weight, increment_coefficients, conv_w, conv_b, dt_bias, decay_rate, gain_out, w_out, w_head):

    def mixer_block(seq_ids, up_index, down_index):
        one_hot_targets = (seq_ids[:, None] == jnp.arange(IDS)[None, :]).astype(jnp.bfloat16)
        embedded = jnp.dot(one_hot_targets, token_embedding_matrix, preferred_element_type=jnp.float32).astype(jnp.bfloat16)
        rescaled_lines = row_norm(embedded.astype(jnp.float32), entry_scale_vector).astype(jnp.bfloat16)
        projected_rows = jnp.dot(rescaled_lines, input_projection_weight, preferred_element_type=jnp.float32).astype(jnp.bfloat16)
        unactivated_step = jnp.dot(rescaled_lines, increment_coefficients, preferred_element_type=jnp.float32)
        gate_part = projected_rows[:, :INNER]
        mixed_in = projected_rows[:, INNER:]
        outputs = []
        for direction, param_index in ((0, up_index), (1, down_index)):
            source = mixed_in if direction == 0 else jnp.flip(mixed_in, 0)
            raw_step = unactivated_step if direction == 0 else jnp.flip(unactivated_step, 0)
            conv_out = filtered_lines(jnp.pad(source, ((KW - 1, 0), (0, 0))), conv_w[param_index], conv_b[param_index])
            step_size = jax.nn.softplus(raw_step + dt_bias[param_index][None, :])
            result = scan_stream(conv_out, step_size, -step_size * decay_rate[param_index][None, :])
            outputs.append(result if direction == 0 else jnp.flip(result, 0))
        gated_out = (outputs[0] + outputs[1]) * jax.nn.silu(gate_part.astype(jnp.float32))
        per_head = gated_out.reshape(-1, HEADS, HEADDIM)
        mean_sq = lax.optimization_barrier(jnp.mean(per_head * per_head, axis=-1, keepdims=True))
        normed_out = (per_head * lax.rsqrt(mean_sq + EPSILON)).reshape(-1, INNER) * gain_out
        return normed_out.astype(jnp.bfloat16)

    def one_sequence(packed):
        seq_tokens, positions, replacement = packed
        seq_ids = seq_tokens.at[positions].set(replacement).astype(jnp.int32)
        masked = jnp.zeros((LENGTH,), jnp.float32).at[positions].set(1.0)
        plus_out = mixer_block(seq_ids, 0, 1)
        minus_out = mixer_block(complement(jnp.flip(seq_ids, 0)), 0, 1)
        combined = (plus_out.astype(jnp.float32) + jnp.flip(minus_out, 0).astype(jnp.float32)).astype(jnp.bfloat16)
        layer_out = jnp.dot(combined, w_out, preferred_element_type=jnp.float32).astype(jnp.bfloat16)
        layer_f32 = layer_out.astype(jnp.float32)
        activated = jax.nn.silu(layer_f32)
        class_scores_raw = jnp.dot(activated, w_head.astype(jnp.float32), precision=lax.Precision.HIGHEST)
        exp_logits = jnp.exp(class_scores_raw)
        prob_rows = exp_logits / lax.optimization_barrier(jnp.sum(exp_logits, axis=-1, keepdims=True))
        target = (seq_tokens[:, None] == jnp.arange(VOCAB)[None, :]).astype(jnp.float32)
        grad_logits = masked[:, None] * (prob_rows - target) / (SEQS * MASKED)
        grad_act = jnp.dot(grad_logits, w_head.astype(jnp.float32).T, precision=lax.Precision.HIGHEST)
        grad_layer = (grad_act * silu_slope(layer_f32)).astype(jnp.bfloat16)
        grad_part = jnp.dot(combined.T, grad_layer, preferred_element_type=jnp.float32)
        return (layer_out, grad_part)
    layers, grads = lax.map(one_sequence, (tokens, mask_pos, replace_ids))
    return (layers, lax.optimization_barrier(jnp.sum(grads, axis=0)))
```

```python
import functools

import jax
import jax.numpy as jnp
from jax import lax
from jax.experimental import pallas as pl
from jax.experimental.pallas import tpu as pltpu
from jax.sharding import PartitionSpec as P

HEADS = 8
HEADDIM = 64
STATE = 64
SPAN = 128
KW = 4
INNER = 512
CONVW = 640
EPSILON = 1e-05
F32 = jnp.float32
BF16 = jnp.bfloat16
HIGH = lax.Precision.HIGHEST
NN = (((1,), (0,)), ((), ()))
NT = (((1,), (1,)), ((), ()))
TN = (((0,), (0,)), ((), ()))


def mm(a, b, dims=NN, precision=None):
    return lax.dot_general(a, b, dims, precision=precision, preferred_element_type=F32)


def split_two(value):
    high = value.astype(BF16)
    return high, (value - high.astype(F32)).astype(BF16)


def eye(rows, cols, dtype=F32):
    return (
        lax.broadcasted_iota(jnp.int32, (rows, cols), 0)
        == lax.broadcasted_iota(jnp.int32, (rows, cols), 1)
    ).astype(dtype)


def silu_half(half):
    return half + half * jnp.tanh(half)


def tables_kernel(
    emb_ref, scale_ref, win_ref, inc_ref, cw_ref, cb_ref, dtb_ref, rate_ref, gain_ref, head_ref,
    conv_out, gate_out, step_out, decay_out, gain_out, head_out,
):
    emb = emb_ref[...].astype(F32)
    none = jnp.zeros((2, emb.shape[1]), F32)
    rows = jnp.concatenate(
        [emb, none, emb[3:4], emb[2:3], emb[1:2], emb[0:1], emb[4:6], none], axis=0
    )
    mean_sq = jnp.mean(rows * rows, axis=-1, keepdims=True)
    normed = (rows * lax.rsqrt(mean_sq + EPSILON) * scale_ref[...]).astype(BF16)
    projected = mm(normed, win_ref[...]).astype(BF16).astype(F32)
    raw = mm(normed, inc_ref[...])
    raw_t = mm(eye(HEADS, HEADS), raw, NT, HIGH)
    dtb_t = mm(eye(HEADS, HEADS), dtb_ref[...], NT, HIGH)
    rate_t = mm(eye(HEADS, HEADS), rate_ref[...], NT, HIGH)
    gate = projected[:, :INNER] * 0.5
    gate_t = jnp.transpose(silu_half(gate))
    mixed = projected[:, INNER:]
    for strand in range(2):
        high, low = split_two(gate_t[:, strand * 8 : strand * 8 + 8])
        gate_out[strand * INNER : (strand + 1) * INNER, :] = jnp.concatenate([high, low], axis=1)
    for side in range(2):
        for strand in range(2):
            param = side ^ strand
            mine = mixed[strand * 8 : strand * 8 + 8]
            taps = [cw_ref[param, j : j + 1, :] * mine for j in range(KW)]
            taps[0] = taps[0] + cb_ref[param : param + 1, :]
            table = jnp.transpose(jnp.concatenate(taps, axis=0) * 0.5)
            high, low = split_two(table)
            conv_out[side, strand * CONVW : (strand + 1) * CONVW, :] = jnp.concatenate(
                [high, low], axis=1
            )
            step = jax.nn.softplus(
                raw_t[:, strand * 8 : strand * 8 + 8] + dtb_t[:, param : param + 1]
            )
            step_out[side, strand] = step
            decay_out[side, strand] = -step * rate_t[:, param : param + 1]
    gain_out[...] = jnp.transpose(jnp.broadcast_to(gain_ref[...], (128, INNER)))
    head_out[...] = mm(eye(8, head_ref.shape[1], BF16), head_ref[...], NT).astype(BF16)


def pick(table, ids):
    total = jnp.zeros((table.shape[0], ids.shape[1]), F32)
    for entry in range(6):
        total = jnp.where(ids == entry, table[:, entry : entry + 1], total)
    return total


def layer_kernel(
    n, length, masked_total,
    tok_ref, pos_ref, rep_ref, conv_ref, gate_ref, step_ref, decay_ref, gain_ref, headt_ref, wout_ref,
    layer_out, send_out, keep_out,
    pos_s, rep_s, ids_s, val_s, step_s, log_s, cum_s, tot_s, scaled_s, state_s, y_s, comb_s,
):
    me = lax.axis_index("seq")
    nb = length // SPAN
    blocks = n * nb
    masks = pos_ref.shape[1]
    wide = pos_s.shape[1]
    unrolled = n <= 16
    rows = 2 * nb * 8

    def loop(count, body):
        if unrolled:
            for k in range(count):
                body(k)
        else:
            pl.loop(0, count)(body)

    pos_s[...] = jnp.full_like(pos_s, -1)
    rep_s[...] = jnp.zeros_like(rep_s)
    pos_s[:, :masks] = pos_ref[...]
    rep_s[:, :masks] = rep_ref[...]
    pos = pos_s[...]
    block_hit = lax.broadcasted_iota(jnp.int32, (blocks, wide), 0) == (pos >> 7)
    put = jnp.where(block_hit, (rep_s[...] + 1).astype(F32), 0.0).astype(BF16)
    lane_hit = (lax.broadcasted_iota(jnp.int32, (SPAN, wide), 0) == (pos & 127)) & (pos >= 0)
    val_s[...] = mm(put, lane_hit.astype(F32).astype(BF16), NT)
    nothing = jnp.full((1, length), -1.0, F32)
    ids_s[0:1, :] = nothing
    ids_s[n + 1 : n + 2, :] = nothing

    def values_of(unit):
        return jnp.concatenate(
            [val_s[pl.ds(unit * nb + b, 1), :] for b in range(nb)], axis=1
        )

    def place(k):
        unit = me ^ k
        put_here = values_of(unit)
        own = tok_ref[pl.ds(k, 1), :].astype(F32)
        ids_s[pl.ds(unit + 1, 1), :] = jnp.where(put_here > 0.5, put_here - 1.0, own)

    loop(n, place)

    lane = lax.broadcasted_iota(jnp.int32, (1, length), 1)
    sub8 = lax.broadcasted_iota(jnp.int32, (8, length), 0).astype(F32)

    def one_hots(unit, side):
        here = ids_s[pl.ds(unit + 1, 1), :]
        beside = ids_s[pl.ds(unit + 2 * side, 1), :]
        out = [(sub8 == here).astype(F32)]
        for j in range(1, KW):
            if isinstance(side, int):
                shift = j if side == 0 else length - j
                border = (lane < j) if side == 0 else (lane >= length - j)
            else:
                shift = jnp.where(side == 0, j, length - j)
                border = jnp.where(side == 0, lane, length - 1 - lane) < j
            moved = jnp.where(
                border, pltpu.roll(beside, shift, 1), pltpu.roll(here, shift, 1)
            )
            out.append((sub8 == moved).astype(F32))
        hot = jnp.concatenate(out, axis=0).astype(BF16)
        return jnp.concatenate([hot, hot], axis=0)

    def slot_of(k):
        before = k < me
        unit = jnp.where(before, me - 1 - k, k + 1)
        side = jnp.where(before, 0, 1)
        return unit, side

    def fill(slot, unit, side):
        here = ids_s[pl.ds(unit + 1, 1), :]
        for source, target in ((step_ref, step_s), (decay_ref, log_s)):
            parts = []
            for strand in range(2):
                full = pick(source[side, strand], here)
                parts += [full[:, b * SPAN : (b + 1) * SPAN] for b in range(nb)]
            target[slot] = jnp.concatenate(parts, axis=0)

    def fill_other(k):
        unit, side = slot_of(k)
        fill(k, unit, side)

    loop(n - 1, fill_other)
    fill(n - 1, me, 0)
    fill(n, me, 1)
    logs = log_s[...].reshape((n + 1) * rows, SPAN)
    before = (
        lax.broadcasted_iota(jnp.int32, (SPAN, SPAN), 0)
        <= lax.broadcasted_iota(jnp.int32, (SPAN, SPAN), 1)
    ).astype(F32)
    cum = mm(logs, before, NN, HIGH).reshape(n + 1, rows, SPAN)
    cum_s[...] = cum
    tot_s[...] = jnp.broadcast_to(cum[:, :, SPAN - 1 :], cum.shape)

    def part(array, strand, b):
        start = (strand * nb + b) * 8
        return array[start : start + 8]

    def weigh(k, far):
        side_back = k >= me
        far = [jnp.where(k == me, 0.0, value) for value in far]
        steps, cums, logs_k, tots = step_s[k], cum_s[k], log_s[k], tot_s[k]
        new = []
        parts = [None] * (2 * nb)
        for strand in range(2):
            whole = sum(part(tots, strand, b) for b in range(nb))
            ahead = jnp.zeros((8, SPAN), F32)
            for b in range(nb):
                behind = whole - ahead - part(tots, strand, b)
                e_fwd = part(tots, strand, b) - part(cums, strand, b) + behind
                e_bwd = part(cums, strand, b) - part(logs_k, strand, b) + ahead
                e = jnp.where(side_back, e_bwd, e_fwd) + far[strand]
                parts[strand * nb + b] = part(steps, strand, b) * jnp.exp(e)
                ahead = ahead + part(tots, strand, b)
            new.append(far[strand] + whole)
        step_s[k] = jnp.concatenate(parts, axis=0)
        return new

    far = [jnp.zeros((8, SPAN), F32)] * 2
    if unrolled:
        for k in range(n - 1):
            far = weigh(k, far)
    else:
        lax.fori_loop(0, n - 1, lambda k, c: tuple(weigh(k, list(c))), tuple(far))

    state_s[...] = jnp.zeros_like(state_s)

    def across(array, strand):
        return jnp.concatenate([part(array, strand, b) for b in range(nb)], axis=1)

    def per_head(x, row8, first):
        return jnp.concatenate(
            [
                x[h * HEADDIM : (h + 1) * HEADDIM] * row8[first + h : first + h + 1]
                for h in range(x.shape[0] // HEADDIM)
            ],
            axis=0,
        )

    def gather_state(k):
        unit, side = slot_of(k)
        hot = one_hots(unit, side)
        weight = step_s[k]
        for strand in range(2):
            row8 = across(weight, strand)
            base = strand * CONVW
            slot = (k * 2 + strand) % 4
            for c in range(4):
                half = mm(conv_ref[side, base + c * 128 : base + (c + 1) * 128, :], hot)
                scaled_s[slot, c * 128 : (c + 1) * 128, :] = per_head(
                    silu_half(half), row8, 2 * c
                ).astype(BF16)
            b_t = silu_half(mm(conv_ref[side, base + INNER : base + INNER + STATE, :], hot))
            state_s[side, strand] += mm(scaled_s[slot], b_t.astype(BF16), NT)

    loop(n - 1, gather_state)

    row_i = lax.broadcasted_iota(jnp.int32, (SPAN, SPAN), 0)
    col_i = lax.broadcasted_iota(jnp.int32, (SPAN, SPAN), 1)
    for side in range(2):
        hot = one_hots(me, side)
        slot = n - 1 + side
        steps, cums, logs_k, tots = step_s[slot], cum_s[slot], log_s[slot], tot_s[slot]
        if side == 1:
            cums = tots - cums + logs_k
        cols = jnp.transpose(cums)
        for strand in range(2):
            base = strand * CONVW
            row8 = across(steps, strand)
            buf = side * 2 + strand
            for c in range(4):
                half = mm(conv_ref[side, base + c * 128 : base + (c + 1) * 128, :], hot)
                scaled_s[buf, c * 128 : (c + 1) * 128, :] = per_head(
                    silu_half(half), row8, 2 * c
                ).astype(BF16)
            bc_t = silu_half(mm(conv_ref[side, base + INNER : base + CONVW, :], hot))
            state = state_s[side, strand]
            for step_index in range(nb):
                b = step_index if side == 0 else nb - 1 - step_index
                at = slice(b * SPAN, (b + 1) * SPAN)
                bc_blk = bc_t[:, at]
                b_rows = jnp.transpose(bc_blk)[:, :STATE].astype(BF16)
                c_t = bc_blk[STATE:].astype(BF16)
                b_t = bc_blk[:STATE].astype(BF16)
                scores = mm(b_rows, c_t)
                causal = (row_i <= col_i) if side == 0 else (row_i >= col_i)
                scores = jnp.where(causal, scores, 0.0)
                cs = part(cums, strand, b)
                tot = part(tots, strand, b)
                carried = mm(state.astype(BF16), c_t)
                grow = jnp.exp(cs)
                for h in range(HEADS):
                    col = (strand * nb + b) * 8 + h
                    e = cs[h : h + 1] - cols[:, col : col + 1]
                    w = (scores * jnp.exp(jnp.minimum(e, 0.0))).astype(BF16)
                    hs = slice(h * HEADDIM, (h + 1) * HEADDIM)
                    y = mm(scaled_s[buf, hs, at], w) + carried[hs] * grow[h : h + 1]
                    if side == 0:
                        y_s[strand, hs, at] = y
                    else:
                        y_s[strand, hs, at] += y
                if step_index < nb - 1:
                    decayed = per_head(
                        scaled_s[buf, :, at].astype(F32), jnp.exp(tot - cs), 0
                    ).astype(BF16)
                    state = per_head(state, jnp.exp(tot)[:, :STATE], 0) + mm(decayed, b_t, NT)

    hot0 = (sub8 == ids_s[pl.ds(me + 1, 1), :]).astype(F32)
    hot0 = jnp.concatenate([hot0, hot0], axis=0).astype(BF16)
    for h in range(HEADS):
        hs = slice(h * HEADDIM, (h + 1) * HEADDIM)
        gain = gain_ref[hs, :]
        gain = jnp.concatenate([gain] * nb, axis=1)
        total = None
        for strand in range(2):
            at = strand * INNER + h * HEADDIM
            g = y_s[strand, hs, :] * mm(gate_ref[at : at + HEADDIM, :], hot0)
            mean_sq = jnp.mean(g * g, axis=0, keepdims=True)
            out = (g * lax.rsqrt(mean_sq + EPSILON) * gain).astype(BF16).astype(F32)
            total = out if total is None else total + out
        comb_s[hs, :] = total.astype(BF16)

    comb_t = comb_s[...]
    comb = jnp.transpose(comb_t.astype(F32)).astype(BF16)
    layer = mm(comb, wout_ref[...]).astype(BF16)
    layer_out[...] = layer
    layer = layer.astype(F32)
    sigma = 0.5 + 0.5 * jnp.tanh(0.5 * layer)
    act_high, act_low = split_two(layer * sigma)
    head_t = headt_ref[...]
    logits = mm(head_t, act_high, NT) + mm(head_t, act_low, NT)
    classes = 5
    real = lax.broadcasted_iota(jnp.int32, (8, length), 0) < classes
    expo = jnp.where(real, jnp.exp(logits), 0.0)
    prob = expo / jnp.sum(expo, axis=0, keepdims=True)
    target = (sub8 == tok_ref[0:1, :].astype(F32)).astype(F32)
    masked = values_of(me) > 0.5
    grad_logits = jnp.where(masked & real, (prob - target) / masked_total, 0.0)
    high, low = split_two(grad_logits)
    both = jnp.concatenate([high.astype(F32), low.astype(F32)], axis=0)
    head2 = jnp.concatenate([head_t.astype(F32)] * 2, axis=0).astype(BF16)
    grad_act = mm(jnp.transpose(both).astype(BF16), head2)
    slope = sigma * (1.0 + layer * (1.0 - sigma))
    grad_layer = (grad_act * slope).astype(BF16)
    core = me % 2
    half = INNER // 2
    send_out[...] = mm(
        comb_s[pl.ds(pl.multiple_of((1 - core) * half, half), half), :], grad_layer
    ).astype(BF16)
    keep_out[...] = mm(
        comb_s[pl.ds(pl.multiple_of(core * half, half), half), :], grad_layer
    ).astype(BF16)


def swap(value, axis, k):
    return lax.ppermute(value, axis, [(i, i ^ k) for i in range(lax.axis_size(axis))])


def strides(n):
    out, stride = [], 2
    while stride < n:
        radix = 4 if n // stride >= 4 else 2
        out.append((stride, radix))
        stride *= radix
    return out


def row_of(stack, index):
    return lax.dynamic_index_in_dim(stack, index, 0, False)


def tree_sum(parts):
    parts = [p.astype(F32) for p in parts]
    while len(parts) > 1:
        parts = [a + b for a, b in zip(parts[::2], parts[1::2])]
    return parts[0].astype(BF16)


def sum_all(send, keep, n):
    core = lax.axis_index("seq") % 2
    mine = lax.axis_index("dp")
    rows, cols = keep.shape
    part = tree_sum([keep, swap(send, "seq", 1)]).reshape(4, rows // 4, cols)
    got = [swap(row_of(part, mine ^ k), "dp", k) for k in (1, 2, 3)]
    part = tree_sum([row_of(part, mine)] + got)
    for stride, radix in strides(n):
        got = [swap(part, "seq", k * stride) for k in range(1, radix)]
        part = tree_sum([part] + got)
    got = [part] + [swap(part, "dp", k) for k in (1, 2, 3)]
    part = jnp.stack(
        [
            jnp.where(mine == j, got[0], jnp.where(mine == j ^ 1, got[1], jnp.where(mine == j ^ 2, got[2], got[3])))
            for j in range(4)
        ]
    ).reshape(rows, cols)
    other = swap(part, "seq", 1)
    low = jnp.where(core == 0, part, other)
    high = jnp.where(core == 0, other, part)
    return jnp.concatenate([low, high], axis=0).astype(F32)


def per_device(
    n, tokens, mask_pos, replace_ids, token_embedding_matrix, entry_scale_vector,
    input_projection_weight, increment_coefficients, conv_w, conv_b, dt_bias, decay_rate,
    gain_out, w_out, w_head,
):
    length = tokens.shape[1]
    width = w_out.shape[1]
    nb = length // SPAN
    rows = 2 * nb * 8
    gathered = jnp.concatenate([tokens, swap(tokens, "seq", 1)], axis=0)
    for stride, radix in strides(n):
        gathered = jnp.concatenate(
            [gathered] + [swap(gathered, "seq", k * stride) for k in range(1, radix)], axis=0
        )
    shape = jax.ShapeDtypeStruct
    tables = pl.pallas_call(
        tables_kernel,
        out_shape=(
            shape((2, 2 * CONVW, 16 * KW), BF16),
            shape((2 * INNER, 16), BF16),
            shape((2, 2, HEADS, 8), F32),
            shape((2, 2, HEADS, 8), F32),
            shape((INNER, 128), F32),
            shape((8, width), BF16),
        ),
        compiler_params=pltpu.CompilerParams(vmem_limit_bytes=32 << 20),
        cost_estimate=pl.CostEstimate(flops=20_000_000, bytes_accessed=3_000_000, transcendentals=10_000),
        name="tables",
    )(
        token_embedding_matrix, entry_scale_vector[None], input_projection_weight,
        increment_coefficients, conv_w, conv_b, dt_bias, decay_rate, gain_out[None], w_head,
    )
    masks = mask_pos.shape[1]
    wide = -(-masks // 128) * 128
    slots = n + 1
    layer_out, send, keep = pl.pallas_call(
        functools.partial(layer_kernel, n, length, lax.axis_size("dp") * masks),
        out_shape=(
            shape((length, width), BF16),
            shape((INNER // 2, width), BF16),
            shape((INNER // 2, width), BF16),
        ),
        scratch_shapes=[
            pltpu.VMEM((1, wide), jnp.int32),
            pltpu.VMEM((1, wide), jnp.int32),
            pltpu.VMEM((n + 2, length), F32),
            pltpu.VMEM((n * nb, SPAN), F32),
            pltpu.VMEM((slots, rows, SPAN), F32),
            pltpu.VMEM((slots, rows, SPAN), F32),
            pltpu.VMEM((slots, rows, SPAN), F32),
            pltpu.VMEM((slots, rows, SPAN), F32),
            pltpu.VMEM((4, INNER, length), BF16),
            pltpu.VMEM((2, 2, INNER, STATE), F32),
            pltpu.VMEM((2, INNER, length), F32),
            pltpu.VMEM((INNER, length), BF16),
        ],
        compiler_params=pltpu.CompilerParams(vmem_limit_bytes=48 << 20),
        cost_estimate=pl.CostEstimate(flops=2_000_000_000, bytes_accessed=4_000_000, transcendentals=4_000_000),
        name="layer",
    )(gathered, mask_pos, replace_ids, *tables, w_out)
    return (layer_out[None], sum_all(send, keep, n))


def solution(mesh):
    in_specs = (P("dp", "seq"), P("dp", None), P("dp", None)) + (P(),) * 11
    out_specs = (P("dp", "seq", None), P())
    return jax.shard_map(
        functools.partial(per_device, mesh.shape["seq"]),
        mesh=mesh, in_specs=in_specs, out_specs=out_specs, check_vma=False,
    )
```

```python
import functools

import jax
import jax.numpy as jnp
from jax import lax
from jax.experimental import pallas as pl
from jax.experimental.pallas import tpu as pltpu
from jax.sharding import PartitionSpec as P

HEADS = 8
HEADDIM = 64
STATE = 64
SPAN = 128
KW = 4
INNER = 512
CONVW = 640
EPSILON = 1e-05
F32 = jnp.float32
BF16 = jnp.bfloat16
HIGH = lax.Precision.HIGHEST
NN = (((1,), (0,)), ((), ()))
NT = (((1,), (1,)), ((), ()))
TN = (((0,), (0,)), ((), ()))


def mm(a, b, dims=NN, precision=None):
    return lax.dot_general(a, b, dims, precision=precision, preferred_element_type=F32)


def split_two(value):
    high = value.astype(BF16)
    return high, (value - high.astype(F32)).astype(BF16)


def eye(rows, cols, dtype=F32):
    return (
        lax.broadcasted_iota(jnp.int32, (rows, cols), 0)
        == lax.broadcasted_iota(jnp.int32, (rows, cols), 1)
    ).astype(dtype)


def silu_half(half):
    return half + half * jnp.tanh(half)


def tables_kernel(*refs):
    count = 10
    sources, outs, buffers, sem = refs[:count], refs[count:-count - 1], refs[-count - 1 : -1], refs[-1]
    copies = [
        pltpu.make_async_copy(source, buffer, sem.at[i])
        for i, (source, buffer) in enumerate(zip(sources, buffers))
    ]
    for copy in copies:
        copy.start()
    for copy in copies:
        copy.wait()
    emb_ref, scale_ref, win_ref, inc_ref, cw_ref, cb_ref, dtb_ref, rate_ref, gain_ref, head_ref = buffers
    conv_out, gate_out, step_out, decay_out, gain_out, head_out = outs
    emb = emb_ref[...].astype(F32)
    none = jnp.zeros((2, emb.shape[1]), F32)
    rows = jnp.concatenate(
        [emb, none, emb[3:4], emb[2:3], emb[1:2], emb[0:1], emb[4:6], none], axis=0
    )
    mean_sq = jnp.mean(rows * rows, axis=-1, keepdims=True)
    normed = (rows * lax.rsqrt(mean_sq + EPSILON) * scale_ref[...]).astype(BF16)
    projected = mm(normed, win_ref[...]).astype(BF16).astype(F32)
    raw_t = mm(inc_ref[...], normed, NT)
    dtb_t = mm(eye(HEADS, HEADS), dtb_ref[...], NT, HIGH)
    rate_t = mm(eye(HEADS, HEADS), rate_ref[...], NT, HIGH)
    gate = projected[:, :INNER] * 0.5
    gate_t = jnp.transpose(silu_half(gate))
    mixed = projected[:, INNER:]
    for strand in range(2):
        high, low = split_two(gate_t[:, strand * 8 : strand * 8 + 8])
        gate_out[strand * INNER : (strand + 1) * INNER, :] = jnp.concatenate([high, low], axis=1)
    for side in range(2):
        for strand in range(2):
            param = side ^ strand
            mine = mixed[strand * 8 : strand * 8 + 8]
            taps = [cw_ref[param, j : j + 1, :] * mine for j in range(KW)]
            taps[0] = taps[0] + cb_ref[param : param + 1, :]
            table = jnp.transpose(jnp.concatenate(taps, axis=0) * 0.5)
            high, low = split_two(table)
            conv_out[side, strand * CONVW : (strand + 1) * CONVW, :] = jnp.concatenate(
                [high, low], axis=1
            )
            step = jax.nn.softplus(
                raw_t[:, strand * 8 : strand * 8 + 8] + dtb_t[:, param : param + 1]
            )
            step_out[side, strand] = step
            decay_out[side, strand] = -step * rate_t[:, param : param + 1]
    gain_out[...] = jnp.transpose(jnp.broadcast_to(gain_ref[...], (128, INNER)))
    classes, width = head_ref.shape
    head_out[...] = jnp.concatenate(
        [head_ref[...].astype(F32), jnp.zeros((8 - classes, width), F32)], axis=0
    ).astype(BF16)


def pick(table, ids):
    total = jnp.zeros((table.shape[0], ids.shape[1]), F32)
    for entry in range(6):
        total = jnp.where(ids == entry, table[:, entry : entry + 1], total)
    return total


def layer_kernel(
    n, length, masked_total,
    tok_ref, pos_ref, rep_ref, conv_ref, gate_ref, step_ref, decay_ref, gain_ref, headt_ref, wout_ref,
    layer_out, send_out, keep_out,
    pos_s, rep_s, ids_s, val_s, step_s, log_s, cum_s, tot_s, scaled_s, state_s, y_s, comb_s,
):
    me = lax.axis_index("seq")
    nb = length // SPAN
    blocks = n * nb
    masks = pos_ref.shape[1]
    wide = pos_s.shape[1]
    unrolled = n <= 16
    rows = 2 * nb * 8

    def loop(count, body):
        if unrolled:
            for k in range(count):
                body(k)
        else:
            pl.loop(0, count)(body)

    pos_s[...] = jnp.full_like(pos_s, -1)
    rep_s[...] = jnp.zeros_like(rep_s)
    pos_s[:, :masks] = pos_ref[...]
    rep_s[:, :masks] = rep_ref[...]
    pos = pos_s[...]
    block_hit = lax.broadcasted_iota(jnp.int32, (blocks, wide), 0) == (pos >> 7)
    put = jnp.where(block_hit, (rep_s[...] + 1).astype(F32), 0.0).astype(BF16)
    lane_hit = (lax.broadcasted_iota(jnp.int32, (SPAN, wide), 0) == (pos & 127)) & (pos >= 0)
    val_s[...] = mm(put, lane_hit.astype(F32).astype(BF16), NT)
    nothing = jnp.full((1, length), -1.0, F32)
    ids_s[0:1, :] = nothing
    ids_s[n + 1 : n + 2, :] = nothing

    def values_of(unit):
        return jnp.concatenate(
            [val_s[pl.ds(unit * nb + b, 1), :] for b in range(nb)], axis=1
        )

    def place(k):
        unit = me ^ k
        put_here = values_of(unit)
        own = tok_ref[pl.ds(k, 1), :]
        ids_s[pl.ds(unit + 1, 1), :] = jnp.where(put_here > 0.5, put_here - 1.0, own)

    loop(n, place)

    lane = lax.broadcasted_iota(jnp.int32, (1, length), 1)
    sub8 = lax.broadcasted_iota(jnp.int32, (8, length), 0).astype(F32)

    def one_hots(unit, side):
        here = ids_s[pl.ds(unit + 1, 1), :]
        beside = ids_s[pl.ds(unit + 2 * side, 1), :]
        out = [(sub8 == here).astype(F32)]
        for j in range(1, KW):
            if isinstance(side, int):
                shift = j if side == 0 else length - j
                border = (lane < j) if side == 0 else (lane >= length - j)
            else:
                shift = jnp.where(side == 0, j, length - j)
                border = jnp.where(side == 0, lane, length - 1 - lane) < j
            moved = jnp.where(
                border, pltpu.roll(beside, shift, 1), pltpu.roll(here, shift, 1)
            )
            out.append((sub8 == moved).astype(F32))
        hot = jnp.concatenate(out, axis=0).astype(BF16)
        return jnp.concatenate([hot, hot], axis=0)

    def slot_of(k):
        before = k < me
        unit = jnp.where(before, me - 1 - k, k + 1)
        side = jnp.where(before, 0, 1)
        return unit, side

    def fill(slot, unit, side):
        here = ids_s[pl.ds(unit + 1, 1), :]
        for source, target in ((step_ref, step_s), (decay_ref, log_s)):
            parts = []
            for strand in range(2):
                full = pick(source[side, strand], here)
                parts += [full[:, b * SPAN : (b + 1) * SPAN] for b in range(nb)]
            target[slot] = jnp.concatenate(parts, axis=0)

    def fill_other(k):
        unit, side = slot_of(k)
        fill(k, unit, side)

    loop(n - 1, fill_other)
    fill(n - 1, me, 0)
    fill(n, me, 1)
    logs = log_s[...].reshape((n + 1) * rows, SPAN)
    before = (
        lax.broadcasted_iota(jnp.int32, (SPAN, SPAN), 0)
        <= lax.broadcasted_iota(jnp.int32, (SPAN, SPAN), 1)
    ).astype(F32)
    cum = mm(logs, before, NN, HIGH).reshape(n + 1, rows, SPAN)
    cum_s[...] = cum
    tot_s[...] = jnp.broadcast_to(cum[:, :, SPAN - 1 :], cum.shape)

    def part(array, strand, b):
        start = (strand * nb + b) * 8
        return array[start : start + 8]

    def weigh(k, far):
        side_back = k >= me
        far = [jnp.where(k == me, 0.0, value) for value in far]
        steps, cums, logs_k, tots = step_s[k], cum_s[k], log_s[k], tot_s[k]
        new = []
        parts = [None] * (2 * nb)
        for strand in range(2):
            whole = sum(part(tots, strand, b) for b in range(nb))
            ahead = jnp.zeros((8, SPAN), F32)
            for b in range(nb):
                behind = whole - ahead - part(tots, strand, b)
                e_fwd = part(tots, strand, b) - part(cums, strand, b) + behind
                e_bwd = part(cums, strand, b) - part(logs_k, strand, b) + ahead
                e = jnp.where(side_back, e_bwd, e_fwd) + far[strand]
                parts[strand * nb + b] = part(steps, strand, b) * jnp.exp(e)
                ahead = ahead + part(tots, strand, b)
            new.append(far[strand] + whole)
        step_s[k] = jnp.concatenate(parts, axis=0)
        return new

    far = [jnp.zeros((8, SPAN), F32)] * 2
    if unrolled:
        for k in range(n - 1):
            far = weigh(k, far)
    else:
        lax.fori_loop(0, n - 1, lambda k, c: tuple(weigh(k, list(c))), tuple(far))

    state_s[...] = jnp.zeros_like(state_s)

    def across(array, strand):
        return jnp.concatenate([part(array, strand, b) for b in range(nb)], axis=1)

    def per_head(x, row8, first):
        return jnp.concatenate(
            [
                x[h * HEADDIM : (h + 1) * HEADDIM] * row8[first + h : first + h + 1]
                for h in range(x.shape[0] // HEADDIM)
            ],
            axis=0,
        )

    def gather_state(k):
        unit, side = slot_of(k)
        hot = one_hots(unit, side)
        weight = step_s[k]
        for strand in range(2):
            row8 = across(weight, strand)
            base = strand * CONVW
            slot = (k * 2 + strand) % 4
            for c in range(4):
                half = mm(conv_ref[side, base + c * 128 : base + (c + 1) * 128, :], hot)
                scaled_s[slot, c * 128 : (c + 1) * 128, :] = per_head(
                    silu_half(half), row8, 2 * c
                ).astype(BF16)
            b_t = silu_half(mm(conv_ref[side, base + INNER : base + INNER + STATE, :], hot))
            state_s[side, strand] += mm(scaled_s[slot], b_t.astype(BF16), NT)

    loop(n - 1, gather_state)

    row_i = lax.broadcasted_iota(jnp.int32, (SPAN, SPAN), 0)
    col_i = lax.broadcasted_iota(jnp.int32, (SPAN, SPAN), 1)
    for side in range(2):
        hot = one_hots(me, side)
        slot = n - 1 + side
        steps, cums, logs_k, tots = step_s[slot], cum_s[slot], log_s[slot], tot_s[slot]
        if side == 1:
            cums = tots - cums + logs_k
        cols = jnp.transpose(cums)
        for strand in range(2):
            base = strand * CONVW
            row8 = across(steps, strand)
            buf = side * 2 + strand
            for c in range(4):
                half = mm(conv_ref[side, base + c * 128 : base + (c + 1) * 128, :], hot)
                scaled_s[buf, c * 128 : (c + 1) * 128, :] = per_head(
                    silu_half(half), row8, 2 * c
                ).astype(BF16)
            bc_t = silu_half(mm(conv_ref[side, base + INNER : base + CONVW, :], hot))
            state = state_s[side, strand]
            for step_index in range(nb):
                b = step_index if side == 0 else nb - 1 - step_index
                at = slice(b * SPAN, (b + 1) * SPAN)
                bc_blk = bc_t[:, at]
                b_rows = jnp.transpose(bc_blk)[:, :STATE].astype(BF16)
                c_t = bc_blk[STATE:].astype(BF16)
                b_t = bc_blk[:STATE].astype(BF16)
                scores = mm(b_rows, c_t)
                causal = (row_i <= col_i) if side == 0 else (row_i >= col_i)
                scores = jnp.where(causal, scores, 0.0)
                cs = part(cums, strand, b)
                tot = part(tots, strand, b)
                carried = mm(state.astype(BF16), c_t)
                grow = jnp.exp(cs)
                for h in range(HEADS):
                    col = (strand * nb + b) * 8 + h
                    e = cs[h : h + 1] - cols[:, col : col + 1]
                    w = (scores * jnp.exp(jnp.minimum(e, 0.0))).astype(BF16)
                    hs = slice(h * HEADDIM, (h + 1) * HEADDIM)
                    y = mm(scaled_s[buf, hs, at], w) + carried[hs] * grow[h : h + 1]
                    if side == 0:
                        y_s[strand, hs, at] = y
                    else:
                        y_s[strand, hs, at] += y
                if step_index < nb - 1:
                    decayed = per_head(
                        scaled_s[buf, :, at].astype(F32), jnp.exp(tot - cs), 0
                    ).astype(BF16)
                    state = per_head(state, jnp.exp(tot)[:, :STATE], 0) + mm(decayed, b_t, NT)

    hot0 = (sub8 == ids_s[pl.ds(me + 1, 1), :]).astype(F32)
    hot0 = jnp.concatenate([hot0, hot0], axis=0).astype(BF16)
    for h in range(HEADS):
        hs = slice(h * HEADDIM, (h + 1) * HEADDIM)
        gain = gain_ref[hs, :]
        gain = jnp.concatenate([gain] * nb, axis=1)
        total = None
        for strand in range(2):
            at = strand * INNER + h * HEADDIM
            g = y_s[strand, hs, :] * mm(gate_ref[at : at + HEADDIM, :], hot0)
            mean_sq = jnp.mean(g * g, axis=0, keepdims=True)
            out = (g * lax.rsqrt(mean_sq + EPSILON) * gain).astype(BF16).astype(F32)
            total = out if total is None else total + out
        comb_s[hs, :] = total.astype(BF16)

    comb_t = comb_s[...]
    comb = jnp.transpose(comb_t.astype(F32)).astype(BF16)
    layer = mm(comb, wout_ref[...]).astype(BF16)
    layer_out[...] = layer
    layer = layer.astype(F32)
    sigma = 0.5 + 0.5 * jnp.tanh(0.5 * layer)
    act_high, act_low = split_two(layer * sigma)
    head_t = headt_ref[...]
    logits = mm(head_t, act_high, NT) + mm(head_t, act_low, NT)
    classes = 5
    real = lax.broadcasted_iota(jnp.int32, (8, length), 0) < classes
    expo = jnp.where(real, jnp.exp(logits), 0.0)
    prob = expo / jnp.sum(expo, axis=0, keepdims=True)
    target = (sub8 == tok_ref[0:1, :]).astype(F32)
    masked = values_of(me) > 0.5
    grad_logits = jnp.where(masked & real, (prob - target) / masked_total, 0.0)
    high, low = split_two(grad_logits)
    both = jnp.concatenate([high.astype(F32), low.astype(F32)], axis=0)
    head2 = jnp.concatenate([head_t.astype(F32)] * 2, axis=0).astype(BF16)
    grad_act = mm(jnp.transpose(both).astype(BF16), head2)
    slope = sigma * (1.0 + layer * (1.0 - sigma))
    grad_layer = (grad_act * slope).astype(BF16)
    core = me % 2
    half = INNER // 2
    send_out[...] = mm(
        comb_s[pl.ds(pl.multiple_of((1 - core) * half, half), half), :], grad_layer
    ).astype(BF16)
    keep_out[...] = mm(
        comb_s[pl.ds(pl.multiple_of(core * half, half), half), :], grad_layer
    ).astype(BF16)


def swap(value, axis, k):
    return lax.ppermute(value, axis, [(i, i ^ k) for i in range(lax.axis_size(axis))])


def strides(n):
    out, stride = [], 2
    while stride < n:
        radix = 4 if n // stride >= 4 else 2
        out.append((stride, radix))
        stride *= radix
    return out


def row_of(stack, index):
    return lax.dynamic_index_in_dim(stack, index, 0, False)


def tree_sum(parts):
    parts = [p.astype(F32) for p in parts]
    while len(parts) > 1:
        parts = [a + b for a, b in zip(parts[::2], parts[1::2])]
    return parts[0].astype(BF16)


def sum_all(send, keep, n):
    core = lax.axis_index("seq") % 2
    mine = lax.axis_index("dp")
    rows, cols = keep.shape
    part = tree_sum([keep, swap(send, "seq", 1)]).reshape(4, rows // 4, cols)
    got = [swap(row_of(part, mine ^ k), "dp", k) for k in (1, 2, 3)]
    part = tree_sum([row_of(part, mine)] + got)
    for stride, radix in strides(n):
        got = [swap(part, "seq", k * stride) for k in range(1, radix)]
        part = tree_sum([part] + got)
    got = [part] + [swap(part, "dp", k) for k in (1, 2, 3)]
    part = jnp.stack(
        [
            jnp.where(mine == j, got[0], jnp.where(mine == j ^ 1, got[1], jnp.where(mine == j ^ 2, got[2], got[3])))
            for j in range(4)
        ]
    ).reshape(rows, cols)
    other = swap(part, "seq", 1)
    low = jnp.where(core == 0, part, other)
    high = jnp.where(core == 0, other, part)
    return jnp.concatenate([low, high], axis=0).astype(F32)


def per_device(
    n, tokens, mask_pos, replace_ids, token_embedding_matrix, entry_scale_vector,
    input_projection_weight, increment_coefficients, conv_w, conv_b, dt_bias, decay_rate,
    gain_out, w_out, w_head,
):
    length = tokens.shape[1]
    width = w_out.shape[1]
    nb = length // SPAN
    rows = 2 * nb * 8
    gathered = jnp.concatenate(
        [tokens.astype(F32), swap(tokens, "seq", 1).astype(F32)], axis=0
    )
    for stride, radix in strides(n):
        gathered = jnp.concatenate(
            [gathered] + [swap(gathered, "seq", k * stride) for k in range(1, radix)], axis=0
        )
    shape = jax.ShapeDtypeStruct
    weights = (
        token_embedding_matrix, entry_scale_vector[None], input_projection_weight,
        increment_coefficients.T, conv_w, conv_b, dt_bias, decay_rate, gain_out[None], w_head.T,
    )
    tables = pl.pallas_call(
        tables_kernel,
        in_specs=[pl.BlockSpec(memory_space=pltpu.HBM)] * len(weights),
        scratch_shapes=[pltpu.VMEM(w.shape, w.dtype) for w in weights]
        + [pltpu.SemaphoreType.DMA((len(weights),))],
        out_shape=(
            pltpu.VMEM((2, 2 * CONVW, 16 * KW), BF16),
            pltpu.VMEM((2 * INNER, 16), BF16),
            pltpu.VMEM((2, 2, HEADS, 8), F32),
            pltpu.VMEM((2, 2, HEADS, 8), F32),
            pltpu.VMEM((INNER, 128), F32),
            pltpu.VMEM((8, width), BF16),
        ),
        compiler_params=pltpu.CompilerParams(vmem_limit_bytes=32 << 20),
        cost_estimate=pl.CostEstimate(flops=20_000_000, bytes_accessed=3_000_000, transcendentals=10_000),
        name="tables",
    )(*[pltpu.with_memory_space_constraint(w, pltpu.HBM) for w in weights])
    masks = mask_pos.shape[1]
    wide = -(-masks // 128) * 128
    slots = n + 1
    operands = (gathered, mask_pos, replace_ids, *tables, w_out)
    layer_out, send, keep = pl.pallas_call(
        functools.partial(layer_kernel, n, length, lax.axis_size("dp") * masks),
        out_shape=(
            shape((length, width), BF16),
            pltpu.VMEM((INNER // 2, width), BF16),
            pltpu.VMEM((INNER // 2, width), BF16),
        ),
        scratch_shapes=[
            pltpu.VMEM((1, wide), jnp.int32),
            pltpu.VMEM((1, wide), jnp.int32),
            pltpu.VMEM((n + 2, length), F32),
            pltpu.VMEM((n * nb, SPAN), F32),
            pltpu.VMEM((slots, rows, SPAN), F32),
            pltpu.VMEM((slots, rows, SPAN), F32),
            pltpu.VMEM((slots, rows, SPAN), F32),
            pltpu.VMEM((slots, rows, SPAN), F32),
            pltpu.VMEM((4, INNER, length), BF16),
            pltpu.VMEM((2, 2, INNER, STATE), F32),
            pltpu.VMEM((2, INNER, length), F32),
            pltpu.VMEM((INNER, length), BF16),
        ],
        compiler_params=pltpu.CompilerParams(vmem_limit_bytes=32 << 20),
        cost_estimate=pl.CostEstimate(flops=2_000_000_000, bytes_accessed=4_000_000, transcendentals=4_000_000),
        name="layer",
    )(*operands)
    return (layer_out[None], sum_all(send, keep, n))


def solution(mesh):
    in_specs = (P("dp", "seq"), P("dp", None), P("dp", None)) + (P(),) * 11
    out_specs = (P("dp", "seq", None), P())
    return jax.shard_map(
        functools.partial(per_device, mesh.shape["seq"]),
        mesh=mesh, in_specs=in_specs, out_specs=out_specs, check_vma=False,
    )
```

```python
import functools

import jax
import jax.numpy as jnp
from jax import lax
from jax.experimental import pallas as pl
from jax.experimental.pallas import tpu as pltpu
from jax.sharding import PartitionSpec as P

HEADS = 8
HEADDIM = 64
STATE = 64
SPAN = 128
KW = 4
INNER = 512
CONVW = 640
EPSILON = 1e-05
F32 = jnp.float32
BF16 = jnp.bfloat16
HIGH = lax.Precision.HIGHEST
NN = (((1,), (0,)), ((), ()))
NT = (((1,), (1,)), ((), ()))
TN = (((0,), (0,)), ((), ()))


def mm(a, b, dims=NN, precision=None):
    return lax.dot_general(a, b, dims, precision=precision, preferred_element_type=F32)


def split_two(value):
    high = value.astype(BF16)
    return high, (value - high.astype(F32)).astype(BF16)


def eye(rows, cols, dtype=F32):
    return (
        lax.broadcasted_iota(jnp.int32, (rows, cols), 0)
        == lax.broadcasted_iota(jnp.int32, (rows, cols), 1)
    ).astype(dtype)


def silu_half(half):
    return half + half * jnp.tanh(half)


def tables_kernel(*refs):
    count = 10
    sources, outs, buffers, sem = refs[:count], refs[count:-count - 1], refs[-count - 1 : -1], refs[-1]
    copies = [
        pltpu.make_async_copy(source, buffer, sem.at[i])
        for i, (source, buffer) in enumerate(zip(sources, buffers))
    ]
    for copy in copies:
        copy.start()
    for copy in copies:
        copy.wait()
    emb_ref, scale_ref, win_ref, inc_ref, cw_ref, cb_ref, dtb_ref, rate_ref, gain_ref, head_ref = buffers
    conv_out, gate_out, step_out, decay_out, gain_out, head_out = outs
    emb = emb_ref[...].astype(F32)
    none = jnp.zeros((2, emb.shape[1]), F32)
    rows = jnp.concatenate(
        [emb, none, emb[3:4], emb[2:3], emb[1:2], emb[0:1], emb[4:6], none], axis=0
    )
    mean_sq = jnp.mean(rows * rows, axis=-1, keepdims=True)
    normed = (rows * lax.rsqrt(mean_sq + EPSILON) * scale_ref[...]).astype(BF16)
    projected = mm(normed, win_ref[...]).astype(BF16).astype(F32)
    raw_t = mm(inc_ref[...], normed, NT)
    dtb_t = mm(eye(HEADS, HEADS), dtb_ref[...], NT, HIGH)
    rate_t = mm(eye(HEADS, HEADS), rate_ref[...], NT, HIGH)
    gate = projected[:, :INNER] * 0.5
    gate_t = jnp.transpose(silu_half(gate))
    mixed = projected[:, INNER:]
    for strand in range(2):
        high, low = split_two(gate_t[:, strand * 8 : strand * 8 + 8])
        gate_out[strand * INNER : (strand + 1) * INNER, :] = jnp.concatenate([high, low], axis=1)
    for side in range(2):
        for strand in range(2):
            param = side ^ strand
            mine = mixed[strand * 8 : strand * 8 + 8]
            taps = [cw_ref[param, j : j + 1, :] * mine for j in range(KW)]
            taps[0] = taps[0] + cb_ref[param : param + 1, :]
            table = jnp.transpose(jnp.concatenate(taps, axis=0) * 0.5)
            high, low = split_two(table)
            conv_out[side, strand * CONVW : (strand + 1) * CONVW, :] = jnp.concatenate(
                [high, low], axis=1
            )
            step = jax.nn.softplus(
                raw_t[:, strand * 8 : strand * 8 + 8] + dtb_t[:, param : param + 1]
            )
            step_out[side, strand] = step
            decay_out[side, strand] = -step * rate_t[:, param : param + 1]
    gain_out[...] = jnp.transpose(jnp.broadcast_to(gain_ref[...], (128, INNER)))
    classes, width = head_ref.shape
    head_out[...] = jnp.concatenate(
        [head_ref[...].astype(F32), jnp.zeros((8 - classes, width), F32)], axis=0
    ).astype(BF16)


def pick(table, ids):
    total = jnp.zeros((table.shape[0], ids.shape[1]), F32)
    for entry in range(6):
        total = jnp.where(ids == entry, table[:, entry : entry + 1], total)
    return total


def layer_kernel(
    n, length, masked_total,
    tok_ref, pos_ref, rep_ref, conv_ref, gate_ref, step_ref, decay_ref, gain_ref, headt_ref, wout_ref,
    layer_out, send_out, keep_out,
    pos_s, rep_s, ids_s, val_s, step_s, log_s, cum_s, tot_s, own_s, from_s, near_s, far_s, farb_s, state_s, y_s, comb_s,
):
    me = lax.axis_index("seq")
    nb = length // SPAN
    blocks = n * nb
    masks = pos_ref.shape[1]
    wide = pos_s.shape[1]
    unrolled = n <= 16
    rows = 2 * nb * 8

    def loop(count, body):
        if unrolled:
            for k in range(count):
                body(k)
        else:
            pl.loop(0, count)(body)

    pos_s[...] = jnp.full_like(pos_s, -1)
    rep_s[...] = jnp.zeros_like(rep_s)
    pos_s[:, :masks] = pos_ref[...]
    rep_s[:, :masks] = rep_ref[...]
    pos = pos_s[...]
    block_hit = lax.broadcasted_iota(jnp.int32, (blocks, wide), 0) == (pos >> 7)
    put = jnp.where(block_hit, (rep_s[...] + 1).astype(F32), 0.0).astype(BF16)
    lane_hit = (lax.broadcasted_iota(jnp.int32, (SPAN, wide), 0) == (pos & 127)) & (pos >= 0)
    val_s[...] = mm(put, lane_hit.astype(F32).astype(BF16), NT)
    nothing = jnp.full((1, length), -1.0, F32)
    ids_s[0:1, :] = nothing
    ids_s[n + 1 : n + 2, :] = nothing

    def values_of(unit):
        return jnp.concatenate(
            [val_s[pl.ds(unit * nb + b, 1), :] for b in range(nb)], axis=1
        )

    def place(k):
        unit = me ^ k
        put_here = values_of(unit)
        own = tok_ref[pl.ds(k, 1), :]
        ids_s[pl.ds(unit + 1, 1), :] = jnp.where(put_here > 0.5, put_here - 1.0, own)

    loop(n, place)

    lane = lax.broadcasted_iota(jnp.int32, (1, length), 1)
    sub8 = lax.broadcasted_iota(jnp.int32, (8, length), 0).astype(F32)

    def one_hots(unit, side):
        here = ids_s[pl.ds(unit + 1, 1), :]
        beside = ids_s[pl.ds(unit + 2 * side, 1), :]
        out = [(sub8 == here).astype(F32)]
        for j in range(1, KW):
            if isinstance(side, int):
                shift = j if side == 0 else length - j
                border = (lane < j) if side == 0 else (lane >= length - j)
            else:
                shift = jnp.where(side == 0, j, length - j)
                border = jnp.where(side == 0, lane, length - 1 - lane) < j
            moved = jnp.where(
                border, pltpu.roll(beside, shift, 1), pltpu.roll(here, shift, 1)
            )
            out.append((sub8 == moved).astype(F32))
        hot = jnp.concatenate(out, axis=0).astype(BF16)
        return jnp.concatenate([hot, hot], axis=0)

    def slot_of(k):
        before = k < me
        unit = jnp.where(before, me - 1 - k, k + 1)
        side = jnp.where(before, 0, 1)
        return unit, side

    def fill(slot, unit, side):
        here = ids_s[pl.ds(unit + 1, 1), :]
        for source, target in ((step_ref, step_s), (decay_ref, log_s)):
            parts = []
            for strand in range(2):
                full = pick(source[side, strand], here)
                parts += [full[:, b * SPAN : (b + 1) * SPAN] for b in range(nb)]
            target[slot] = jnp.concatenate(parts, axis=0)

    def fill_other(k):
        unit, side = slot_of(k)
        fill(k, unit, side)

    loop(n - 1, fill_other)
    fill(n - 1, me, 0)
    fill(n, me, 1)
    logs = log_s[...].reshape((n + 1) * rows, SPAN)
    before = (
        lax.broadcasted_iota(jnp.int32, (SPAN, SPAN), 0)
        <= lax.broadcasted_iota(jnp.int32, (SPAN, SPAN), 1)
    ).astype(F32)
    cum = mm(logs, before, NN, HIGH).reshape(n + 1, rows, SPAN)
    cum_s[...] = cum
    tot_s[...] = jnp.broadcast_to(cum[:, :, SPAN - 1 :], cum.shape)

    def part(array, strand, b):
        start = (strand * nb + b) * 8
        return array[start : start + 8]

    def weigh(k, far):
        side_back = k >= me
        far = [jnp.where(k == me, 0.0, value) for value in far]
        steps, cums, logs_k, tots = step_s[k], cum_s[k], log_s[k], tot_s[k]
        new = []
        parts = [None] * (2 * nb)
        for strand in range(2):
            whole = sum(part(tots, strand, b) for b in range(nb))
            ahead = jnp.zeros((8, SPAN), F32)
            for b in range(nb):
                behind = whole - ahead - part(tots, strand, b)
                e_fwd = part(tots, strand, b) - part(cums, strand, b) + behind
                e_bwd = part(cums, strand, b) - part(logs_k, strand, b) + ahead
                e = jnp.where(side_back, e_bwd, e_fwd) + far[strand]
                parts[strand * nb + b] = part(steps, strand, b) * jnp.exp(e)
                ahead = ahead + part(tots, strand, b)
            new.append(far[strand] + whole)
        step_s[k] = jnp.concatenate(parts, axis=0)
        return new

    far = [jnp.zeros((8, SPAN), F32)] * 2
    if unrolled:
        for k in range(n - 1):
            far = weigh(k, far)
    else:
        lax.fori_loop(0, n - 1, lambda k, c: tuple(weigh(k, list(c))), tuple(far))

    def across(array, strand):
        return jnp.concatenate([part(array, strand, b) for b in range(nb)], axis=1)

    def per_head(x, row8, first):
        return jnp.concatenate(
            [
                x[h * HEADDIM : (h + 1) * HEADDIM] * row8[first + h : first + h + 1]
                for h in range(x.shape[0] // HEADDIM)
            ],
            axis=0,
        )

    def gather_state(k, spot):
        unit, side = slot_of(k)
        hot = one_hots(unit, side)
        weight = step_s[k]
        at = slice(spot * length, (spot + 1) * length)
        for strand in range(2):
            row8 = across(weight, strand)
            base = strand * CONVW
            for c in range(4):
                half = mm(conv_ref[side, base + c * 128 : base + (c + 1) * 128, :], hot)
                far_s[strand, c * 128 : (c + 1) * 128, at] = per_head(
                    silu_half(half), row8, 2 * c
                ).astype(BF16)
            b_t = silu_half(mm(conv_ref[side, base + INNER : base + INNER + STATE, :], hot))
            farb_s[strand, :STATE, at] = jnp.where(side == 0, b_t, 0.0).astype(BF16)
            farb_s[strand, STATE:, at] = jnp.where(side == 0, 0.0, b_t).astype(BF16)

    if unrolled:
        for k in range(n - 1):
            gather_state(k, k)
        for strand in range(2):
            state_s[strand] = mm(far_s[strand], farb_s[strand], NT)
    else:
        state_s[...] = jnp.zeros_like(state_s)

        def add_state(k):
            gather_state(k, 0)
            for strand in range(2):
                state_s[strand] += mm(far_s[strand], farb_s[strand], NT)

        loop(n - 1, add_state)

    row_i = lax.broadcasted_iota(jnp.int32, (SPAN, SPAN), 0)
    col_i = lax.broadcasted_iota(jnp.int32, (SPAN, SPAN), 1)
    sides = []
    for side in range(2):
        slot = n - 1 + side
        steps, cums, logs_k, tots = step_s[slot], cum_s[slot], log_s[slot], tot_s[slot]
        if side == 1:
            cums = tots - cums + logs_k
        sides.append((one_hots(me, side), steps, cums, tots, jnp.transpose(cums)))
    for strand in range(2):
        base = strand * CONVW
        states = state_s[strand].astype(BF16)
        scores, grown, near = {}, {}, {}
        for side in range(2):
            hot, steps, cums, tots, _ = sides[side]
            row8 = across(steps, strand)
            for c in range(4):
                half = mm(conv_ref[side, base + c * 128 : base + (c + 1) * 128, :], hot)
                x = per_head(silu_half(half), row8, 2 * c).astype(BF16)
                for b in range(nb):
                    to = (b * 2 + side) * SPAN
                    own_s[strand, c * 128 : (c + 1) * 128, to : to + SPAN] = x[:, b * SPAN : (b + 1) * SPAN]
            bc_t = silu_half(mm(conv_ref[side, base + INNER : base + CONVW, :], hot))
            c_only = bc_t[STATE:]
            none = jnp.zeros_like(c_only)
            c_both = jnp.concatenate([c_only, none] if side == 0 else [none, c_only], axis=0)
            from_s[strand, side] = mm(states, c_both.astype(BF16))
            c_t, b_t = c_only.astype(BF16), bc_t[:STATE].astype(BF16)
            ahead = jnp.zeros((8, SPAN), F32)
            local = None
            for step_index in range(nb):
                b = step_index if side == 0 else nb - 1 - step_index
                at = slice(b * SPAN, (b + 1) * SPAN)
                b_rows = jnp.transpose(bc_t[:, at])[:, :STATE].astype(BF16)
                causal = (row_i <= col_i) if side == 0 else (row_i >= col_i)
                scores[side, b] = jnp.where(causal, mm(b_rows, c_t[:, at]), 0.0)
                cs, tot = part(cums, strand, b), part(tots, strand, b)
                grown[side, b] = (jnp.exp(cs), jnp.exp(cs + ahead))
                near[side, b] = local is not None
                if local is not None:
                    near_s[strand, side, :, at] = mm(local.astype(BF16), c_t[:, at])
                if step_index < nb - 1:
                    to = (b * 2 + side) * SPAN
                    decayed = per_head(
                        own_s[strand, :, to : to + SPAN].astype(F32), jnp.exp(tot - cs), 0
                    ).astype(BF16)
                    fresh = mm(decayed, b_t[:, at], NT)
                    if local is not None:
                        fresh = fresh + per_head(local, jnp.exp(tot)[:, :STATE], 0)
                    local = fresh
                    ahead = ahead + tot
        for b in range(nb):
            at = slice(b * SPAN, (b + 1) * SPAN)
            for h in range(HEADS):
                hs = slice(h * HEADDIM, (h + 1) * HEADDIM)
                both = []
                for side in range(2):
                    col = (strand * nb + b) * 8 + h
                    e = part(sides[side][2], strand, b)[h : h + 1] - sides[side][4][:, col : col + 1]
                    both.append((scores[side, b] * jnp.exp(jnp.minimum(e, 0.0))).astype(BF16))
                y = mm(
                    own_s[strand, hs, b * 2 * SPAN : (b + 1) * 2 * SPAN],
                    jnp.concatenate(both, axis=0),
                )
                for side in range(2):
                    here, far_grow = grown[side, b]
                    y = y + from_s[strand, side, hs, at] * far_grow[h : h + 1]
                    if near[side, b]:
                        y = y + near_s[strand, side, hs, at] * here[h : h + 1]
                y_s[strand, hs, at] = y

    hot0 = (sub8 == ids_s[pl.ds(me + 1, 1), :]).astype(F32)
    hot0 = jnp.concatenate([hot0, hot0], axis=0).astype(BF16)
    for h in range(HEADS):
        hs = slice(h * HEADDIM, (h + 1) * HEADDIM)
        gain = gain_ref[hs, :]
        gain = jnp.concatenate([gain] * nb, axis=1)
        total = None
        for strand in range(2):
            at = strand * INNER + h * HEADDIM
            g = y_s[strand, hs, :] * mm(gate_ref[at : at + HEADDIM, :], hot0)
            mean_sq = jnp.mean(g * g, axis=0, keepdims=True)
            out = (g * lax.rsqrt(mean_sq + EPSILON) * gain).astype(BF16).astype(F32)
            total = out if total is None else total + out
        comb_s[hs, :] = total.astype(BF16)

    comb_t = comb_s[...]
    comb = jnp.transpose(comb_t.astype(F32)).astype(BF16)
    layer = mm(comb, wout_ref[...]).astype(BF16)
    layer_out[...] = layer
    layer = layer.astype(F32)
    sigma = 0.5 + 0.5 * jnp.tanh(0.5 * layer)
    act_high, act_low = split_two(layer * sigma)
    head_t = headt_ref[...]
    logits = mm(head_t, act_high, NT) + mm(head_t, act_low, NT)
    classes = 5
    real = lax.broadcasted_iota(jnp.int32, (8, length), 0) < classes
    expo = jnp.where(real, jnp.exp(logits), 0.0)
    prob = expo / jnp.sum(expo, axis=0, keepdims=True)
    target = (sub8 == tok_ref[0:1, :]).astype(F32)
    masked = values_of(me) > 0.5
    grad_logits = jnp.where(masked & real, (prob - target) / masked_total, 0.0)
    high, low = split_two(grad_logits)
    both = jnp.concatenate([high.astype(F32), low.astype(F32)], axis=0)
    head2 = jnp.concatenate([head_t.astype(F32)] * 2, axis=0).astype(BF16)
    grad_act = mm(jnp.transpose(both).astype(BF16), head2)
    slope = sigma * (1.0 + layer * (1.0 - sigma))
    grad_layer = (grad_act * slope).astype(BF16)
    core = me % 2
    half = INNER // 2
    send_out[...] = mm(
        comb_s[pl.ds(pl.multiple_of((1 - core) * half, half), half), :], grad_layer
    ).astype(BF16)
    keep_out[...] = mm(
        comb_s[pl.ds(pl.multiple_of(core * half, half), half), :], grad_layer
    ).astype(BF16)


def swap(value, axis, k):
    return lax.ppermute(value, axis, [(i, i ^ k) for i in range(lax.axis_size(axis))])


def strides(n):
    out, stride = [], 2
    while stride < n:
        radix = 4 if n // stride >= 4 else 2
        out.append((stride, radix))
        stride *= radix
    return out


def row_of(stack, index):
    return lax.dynamic_index_in_dim(stack, index, 0, False)


def tree_sum(parts):
    parts = [p.astype(F32) for p in parts]
    while len(parts) > 1:
        parts = [a + b for a, b in zip(parts[::2], parts[1::2])]
    return parts[0].astype(BF16)


def sum_all(send, keep, n):
    core = lax.axis_index("seq") % 2
    mine = lax.axis_index("dp")
    rows, cols = keep.shape
    part = tree_sum([keep, swap(send, "seq", 1)]).reshape(4, rows // 4, cols)
    got = [swap(row_of(part, mine ^ k), "dp", k) for k in (1, 2, 3)]
    part = tree_sum([row_of(part, mine)] + got)
    for stride, radix in strides(n):
        got = [swap(part, "seq", k * stride) for k in range(1, radix)]
        part = tree_sum([part] + got)
    got = [part] + [swap(part, "dp", k) for k in (1, 2, 3)]
    part = jnp.stack(
        [
            jnp.where(mine == j, got[0], jnp.where(mine == j ^ 1, got[1], jnp.where(mine == j ^ 2, got[2], got[3])))
            for j in range(4)
        ]
    ).reshape(rows, cols)
    other = swap(part, "seq", 1)
    low = jnp.where(core == 0, part, other)
    high = jnp.where(core == 0, other, part)
    return jnp.concatenate([low, high], axis=0).astype(F32)


def per_device(
    n, tokens, mask_pos, replace_ids, token_embedding_matrix, entry_scale_vector,
    input_projection_weight, increment_coefficients, conv_w, conv_b, dt_bias, decay_rate,
    gain_out, w_out, w_head,
):
    length = tokens.shape[1]
    width = w_out.shape[1]
    nb = length // SPAN
    rows = 2 * nb * 8
    gathered = jnp.concatenate(
        [tokens.astype(F32), swap(tokens, "seq", 1).astype(F32)], axis=0
    )
    for stride, radix in strides(n):
        gathered = jnp.concatenate(
            [gathered] + [swap(gathered, "seq", k * stride) for k in range(1, radix)], axis=0
        )
    shape = jax.ShapeDtypeStruct
    weights = (
        token_embedding_matrix, entry_scale_vector[None], input_projection_weight,
        increment_coefficients.T, conv_w, conv_b, dt_bias, decay_rate, gain_out[None], w_head.T,
    )
    tables = pl.pallas_call(
        tables_kernel,
        in_specs=[pl.BlockSpec(memory_space=pltpu.HBM)] * len(weights),
        scratch_shapes=[pltpu.VMEM(w.shape, w.dtype) for w in weights]
        + [pltpu.SemaphoreType.DMA((len(weights),))],
        out_shape=(
            pltpu.VMEM((2, 2 * CONVW, 16 * KW), BF16),
            pltpu.VMEM((2 * INNER, 16), BF16),
            pltpu.VMEM((2, 2, HEADS, 8), F32),
            pltpu.VMEM((2, 2, HEADS, 8), F32),
            pltpu.VMEM((INNER, 128), F32),
            pltpu.VMEM((8, width), BF16),
        ),
        compiler_params=pltpu.CompilerParams(vmem_limit_bytes=32 << 20),
        cost_estimate=pl.CostEstimate(flops=20_000_000, bytes_accessed=3_000_000, transcendentals=10_000),
        name="tables",
    )(*[pltpu.with_memory_space_constraint(w, pltpu.HBM) for w in weights])
    masks = mask_pos.shape[1]
    wide = -(-masks // 128) * 128
    slots = n + 1
    spots = n - 1 if n <= 16 else 1
    operands = (gathered, mask_pos, replace_ids, *tables, w_out)
    layer_out, send, keep = pl.pallas_call(
        functools.partial(layer_kernel, n, length, lax.axis_size("dp") * masks),
        out_shape=(
            shape((length, width), BF16),
            pltpu.VMEM((INNER // 2, width), BF16),
            pltpu.VMEM((INNER // 2, width), BF16),
        ),
        scratch_shapes=[
            pltpu.VMEM((1, wide), jnp.int32),
            pltpu.VMEM((1, wide), jnp.int32),
            pltpu.VMEM((n + 2, length), F32),
            pltpu.VMEM((n * nb, SPAN), F32),
            pltpu.VMEM((slots, rows, SPAN), F32),
            pltpu.VMEM((slots, rows, SPAN), F32),
            pltpu.VMEM((slots, rows, SPAN), F32),
            pltpu.VMEM((slots, rows, SPAN), F32),
            pltpu.VMEM((2, INNER, 2 * length), BF16),
            pltpu.VMEM((2, 2, INNER, length), F32),
            pltpu.VMEM((2, 2, INNER, length), F32),
            pltpu.VMEM((2, INNER, spots * length), BF16),
            pltpu.VMEM((2, 2 * STATE, spots * length), BF16),
            pltpu.VMEM((2, INNER, 2 * STATE), F32),
            pltpu.VMEM((2, INNER, length), F32),
            pltpu.VMEM((INNER, length), BF16),
        ],
        compiler_params=pltpu.CompilerParams(vmem_limit_bytes=32 << 20),
        cost_estimate=pl.CostEstimate(flops=2_000_000_000, bytes_accessed=4_000_000, transcendentals=4_000_000),
        name="layer",
    )(*operands)
    return (layer_out[None], sum_all(send, keep, n))


def solution(mesh):
    in_specs = (P("dp", "seq"), P("dp", None), P("dp", None)) + (P(),) * 11
    out_specs = (P("dp", "seq", None), P())
    return jax.shard_map(
        functools.partial(per_device, mesh.shape["seq"]),
        mesh=mesh, in_specs=in_specs, out_specs=out_specs, check_vma=False,
    )
```

```python
import functools

import jax
import jax.numpy as jnp
from jax import lax
from jax.experimental import pallas as pl
from jax.experimental.pallas import tpu as pltpu
from jax.sharding import PartitionSpec as P

HEADS = 8
HEADDIM = 64
STATE = 64
SPAN = 128
KW = 4
INNER = 512
CONVW = 640
EPSILON = 1e-05
F32 = jnp.float32
BF16 = jnp.bfloat16
HIGH = lax.Precision.HIGHEST
NN = (((1,), (0,)), ((), ()))
NT = (((1,), (1,)), ((), ()))
TN = (((0,), (0,)), ((), ()))


def mm(a, b, dims=NN, precision=None):
    return lax.dot_general(a, b, dims, precision=precision, preferred_element_type=F32)


def split_two(value):
    high = value.astype(BF16)
    return high, (value - high.astype(F32)).astype(BF16)


def eye(rows, cols, dtype=F32):
    return (
        lax.broadcasted_iota(jnp.int32, (rows, cols), 0)
        == lax.broadcasted_iota(jnp.int32, (rows, cols), 1)
    ).astype(dtype)


def silu_half(half):
    return half + half * jnp.tanh(half)


def tables_kernel(*refs):
    count = 13
    sources, outs, buffers = refs[:count], refs[count : count + 7], refs[count + 7 : 2 * count + 7]
    pos_s, rep_s, sem = refs[2 * count + 7 :]
    copies = [
        pltpu.make_async_copy(source, buffer, sem.at[i])
        for i, (source, buffer) in enumerate(zip(sources, buffers))
    ]
    for copy in copies:
        copy.start()
    for copy in copies:
        copy.wait()
    (
        emb_ref, scale_ref, win_ref, inc_ref, cw_ref, cb_ref, dtb_ref, rate_ref, gain_ref, head_ref,
        tok_ref, pos_ref, rep_ref,
    ) = buffers
    conv_out, gate_out, step_out, decay_out, gain_out, head_out, val_out = outs

    masks, wide, blocks = pos_ref.shape[1], pos_s.shape[1], val_out.shape[0]
    pos_s[...] = jnp.full_like(pos_s, -1)
    rep_s[...] = jnp.zeros_like(rep_s)
    pos_s[:, :masks] = pos_ref[...]
    rep_s[:, :masks] = rep_ref[...]
    pos = pos_s[...]
    block_hit = lax.broadcasted_iota(jnp.int32, (blocks, wide), 0) == (pos >> 7)
    put = jnp.where(block_hit, (rep_s[...] + 1).astype(F32), 0.0).astype(BF16)
    lane_hit = (lax.broadcasted_iota(jnp.int32, (SPAN, wide), 0) == (pos & 127)) & (pos >= 0)
    val_out[...] = mm(put, lane_hit.astype(F32).astype(BF16), NT)
    length = tok_ref.shape[1]
    nb = length // SPAN
    first = lax.axis_index("seq") * nb
    val = jnp.concatenate([val_out[pl.ds(first + b, 1), :] for b in range(nb)], axis=1)
    ids = jnp.where(val > 0.5, val - 1.0, tok_ref[...].astype(F32))
    hot = (lax.broadcasted_iota(jnp.int32, (8, length), 0).astype(F32) == ids).astype(F32)
    hot = jnp.concatenate([hot, hot], axis=0).astype(BF16)
    emb = emb_ref[...].astype(F32)
    none = jnp.zeros((2, emb.shape[1]), F32)
    rows = jnp.concatenate(
        [emb, none, emb[3:4], emb[2:3], emb[1:2], emb[0:1], emb[4:6], none], axis=0
    )
    mean_sq = jnp.mean(rows * rows, axis=-1, keepdims=True)
    normed = (rows * lax.rsqrt(mean_sq + EPSILON) * scale_ref[...]).astype(BF16)
    projected = mm(normed, win_ref[...]).astype(BF16).astype(F32)
    raw_t = mm(inc_ref[...], normed, NT)
    dtb_t = mm(eye(HEADS, HEADS), dtb_ref[...], NT, HIGH)
    rate_t = mm(eye(HEADS, HEADS), rate_ref[...], NT, HIGH)
    gate = projected[:, :INNER] * 0.5
    gate_t = jnp.transpose(silu_half(gate))
    mixed = projected[:, INNER:]
    for strand in range(2):
        high, low = split_two(gate_t[:, strand * 8 : strand * 8 + 8])
        gate_out[strand * INNER : (strand + 1) * INNER, :] = mm(jnp.concatenate([high, low], axis=1), hot)
    for side in range(2):
        for strand in range(2):
            param = side ^ strand
            mine = mixed[strand * 8 : strand * 8 + 8]
            taps = [cw_ref[param, j : j + 1, :] * mine for j in range(KW)]
            taps[0] = taps[0] + cb_ref[param : param + 1, :]
            table = jnp.transpose(jnp.concatenate(taps, axis=0) * 0.5)
            high, low = split_two(table)
            conv_out[side, strand * CONVW : (strand + 1) * CONVW, :] = jnp.concatenate(
                [high, low], axis=1
            )
            step = jax.nn.softplus(
                raw_t[:, strand * 8 : strand * 8 + 8] + dtb_t[:, param : param + 1]
            )
            step_out[side, strand] = step
            decay_out[side, strand] = -step * rate_t[:, param : param + 1]
    gain_out[...] = jnp.transpose(jnp.broadcast_to(gain_ref[...], (128, INNER)))
    classes, width = head_ref.shape
    head_out[...] = jnp.concatenate(
        [head_ref[...].astype(F32), jnp.zeros((8 - classes, width), F32)], axis=0
    ).astype(BF16)


def pick(table, ids):
    total = jnp.zeros((table.shape[0], ids.shape[1]), F32)
    for entry in range(6):
        total = jnp.where(ids == entry, table[:, entry : entry + 1], total)
    return total


def layer_kernel(
    n, length, masked_total,
    tok_ref, conv_ref, gate_ref, step_ref, decay_ref, gain_ref, headt_ref, val_s, wout_ref,
    layer_out, send_out, keep_out,
    ids_s, step_s, log_s, cum_s, tot_s, own_s, from_s, near_s, far_s, farb_s, state_s, y_s, comb_s,
):
    me = lax.axis_index("seq")
    nb = length // SPAN
    unrolled = n <= 16
    rows = 2 * nb * 8

    def loop(count, body):
        if unrolled:
            for k in range(count):
                body(k)
        else:
            pl.loop(0, count)(body)

    nothing = jnp.full((1, length), -1.0, F32)
    ids_s[0:1, :] = nothing
    ids_s[n + 1 : n + 2, :] = nothing

    def values_of(unit):
        return jnp.concatenate(
            [val_s[pl.ds(unit * nb + b, 1), :] for b in range(nb)], axis=1
        )

    def place(k):
        unit = me ^ k
        put_here = values_of(unit)
        own = tok_ref[pl.ds(k, 1), :]
        ids_s[pl.ds(unit + 1, 1), :] = jnp.where(put_here > 0.5, put_here - 1.0, own)

    loop(n, place)

    lane = lax.broadcasted_iota(jnp.int32, (1, length), 1)
    sub8 = lax.broadcasted_iota(jnp.int32, (8, length), 0).astype(F32)

    def one_hots(unit, side):
        here = ids_s[pl.ds(unit + 1, 1), :]
        beside = ids_s[pl.ds(unit + 2 * side, 1), :]
        out = [(sub8 == here).astype(F32)]
        for j in range(1, KW):
            if isinstance(side, int):
                shift = j if side == 0 else length - j
                border = (lane < j) if side == 0 else (lane >= length - j)
            else:
                shift = jnp.where(side == 0, j, length - j)
                border = jnp.where(side == 0, lane, length - 1 - lane) < j
            moved = jnp.where(
                border, pltpu.roll(beside, shift, 1), pltpu.roll(here, shift, 1)
            )
            out.append((sub8 == moved).astype(F32))
        hot = jnp.concatenate(out, axis=0).astype(BF16)
        return jnp.concatenate([hot, hot], axis=0)

    def slot_of(k):
        before = k < me
        unit = jnp.where(before, me - 1 - k, k + 1)
        side = jnp.where(before, 0, 1)
        return unit, side

    def fill(slot, unit, side):
        here = ids_s[pl.ds(unit + 1, 1), :]
        for source, target in ((step_ref, step_s), (decay_ref, log_s)):
            parts = []
            for strand in range(2):
                full = pick(source[side, strand], here)
                parts += [full[:, b * SPAN : (b + 1) * SPAN] for b in range(nb)]
            target[slot] = jnp.concatenate(parts, axis=0)

    def fill_other(k):
        unit, side = slot_of(k)
        fill(k, unit, side)

    loop(n - 1, fill_other)
    fill(n - 1, me, 0)
    fill(n, me, 1)
    logs = log_s[...].reshape((n + 1) * rows, SPAN)
    before = (
        lax.broadcasted_iota(jnp.int32, (SPAN, SPAN), 0)
        <= lax.broadcasted_iota(jnp.int32, (SPAN, SPAN), 1)
    ).astype(F32)
    cum = mm(logs, before, NN, HIGH).reshape(n + 1, rows, SPAN)
    cum_s[...] = cum
    tot_s[...] = jnp.broadcast_to(cum[:, :, SPAN - 1 :], cum.shape)

    def part(array, strand, b):
        start = (strand * nb + b) * 8
        return array[start : start + 8]

    def weigh(k, far):
        side_back = k >= me
        far = [jnp.where(k == me, 0.0, value) for value in far]
        steps, cums, logs_k, tots = step_s[k], cum_s[k], log_s[k], tot_s[k]
        new = []
        parts = [None] * (2 * nb)
        for strand in range(2):
            whole = sum(part(tots, strand, b) for b in range(nb))
            ahead = jnp.zeros((8, SPAN), F32)
            for b in range(nb):
                behind = whole - ahead - part(tots, strand, b)
                e_fwd = part(tots, strand, b) - part(cums, strand, b) + behind
                e_bwd = part(cums, strand, b) - part(logs_k, strand, b) + ahead
                e = jnp.where(side_back, e_bwd, e_fwd) + far[strand]
                parts[strand * nb + b] = part(steps, strand, b) * jnp.exp(e)
                ahead = ahead + part(tots, strand, b)
            new.append(far[strand] + whole)
        step_s[k] = jnp.concatenate(parts, axis=0)
        return new

    far = [jnp.zeros((8, SPAN), F32)] * 2
    if unrolled:
        for k in range(n - 1):
            far = weigh(k, far)
    else:
        lax.fori_loop(0, n - 1, lambda k, c: tuple(weigh(k, list(c))), tuple(far))

    def across(array, strand):
        return jnp.concatenate([part(array, strand, b) for b in range(nb)], axis=1)

    def per_head(x, row8, first):
        return jnp.concatenate(
            [
                x[h * HEADDIM : (h + 1) * HEADDIM] * row8[first + h : first + h + 1]
                for h in range(x.shape[0] // HEADDIM)
            ],
            axis=0,
        )

    def gather_state(k, spot):
        unit, side = slot_of(k)
        hot = one_hots(unit, side)
        weight = step_s[k]
        at = slice(spot * length, (spot + 1) * length)
        for strand in range(2):
            row8 = across(weight, strand)
            base = strand * CONVW
            for c in range(4):
                half = mm(conv_ref[side, base + c * 128 : base + (c + 1) * 128, :], hot).astype(BF16)
                far_s[strand, c * 128 : (c + 1) * 128, at] = per_head(
                    silu_half(half), row8.astype(BF16), 2 * c
                )
            b_t = silu_half(mm(conv_ref[side, base + INNER : base + INNER + STATE, :], hot))
            farb_s[strand, :STATE, at] = jnp.where(side == 0, b_t, 0.0).astype(BF16)
            farb_s[strand, STATE:, at] = jnp.where(side == 0, 0.0, b_t).astype(BF16)

    if unrolled:
        for k in range(n - 1):
            gather_state(k, k)
        for strand in range(2):
            state_s[strand] = mm(far_s[strand], farb_s[strand], NT)
    else:
        state_s[...] = jnp.zeros_like(state_s)

        def add_state(k):
            gather_state(k, 0)
            for strand in range(2):
                state_s[strand] += mm(far_s[strand], farb_s[strand], NT)

        loop(n - 1, add_state)

    row_i = lax.broadcasted_iota(jnp.int32, (SPAN, SPAN), 0)
    col_i = lax.broadcasted_iota(jnp.int32, (SPAN, SPAN), 1)
    sides = []
    for side in range(2):
        slot = n - 1 + side
        steps, cums, logs_k, tots = step_s[slot], cum_s[slot], log_s[slot], tot_s[slot]
        if side == 1:
            cums = tots - cums + logs_k
        sides.append((one_hots(me, side), steps, cums, tots, jnp.transpose(cums)))
    for strand in range(2):
        base = strand * CONVW
        states = state_s[strand].astype(BF16)
        scores, grown, near = {}, {}, {}
        for side in range(2):
            hot, steps, cums, tots, _ = sides[side]
            row8 = across(steps, strand)
            for c in range(4):
                half = mm(conv_ref[side, base + c * 128 : base + (c + 1) * 128, :], hot)
                x = per_head(silu_half(half), row8, 2 * c).astype(BF16)
                for b in range(nb):
                    to = (b * 2 + side) * SPAN
                    own_s[strand, c * 128 : (c + 1) * 128, to : to + SPAN] = x[:, b * SPAN : (b + 1) * SPAN]
            bc_t = silu_half(mm(conv_ref[side, base + INNER : base + CONVW, :], hot))
            c_only = bc_t[STATE:]
            none = jnp.zeros_like(c_only)
            c_both = jnp.concatenate([c_only, none] if side == 0 else [none, c_only], axis=0)
            from_s[strand, side] = mm(states, c_both.astype(BF16))
            c_t, b_t = c_only.astype(BF16), bc_t[:STATE].astype(BF16)
            ahead = jnp.zeros((8, SPAN), F32)
            local = None
            for step_index in range(nb):
                b = step_index if side == 0 else nb - 1 - step_index
                at = slice(b * SPAN, (b + 1) * SPAN)
                b_rows = jnp.transpose(bc_t[:, at])[:, :STATE].astype(BF16)
                causal = (row_i <= col_i) if side == 0 else (row_i >= col_i)
                scores[side, b] = jnp.where(causal, mm(b_rows, c_t[:, at]), 0.0)
                cs, tot = part(cums, strand, b), part(tots, strand, b)
                grown[side, b] = (jnp.exp(cs), jnp.exp(cs + ahead))
                near[side, b] = local is not None
                if local is not None:
                    near_s[strand, side, :, at] = mm(local.astype(BF16), c_t[:, at])
                if step_index < nb - 1:
                    to = (b * 2 + side) * SPAN
                    decayed = per_head(
                        own_s[strand, :, to : to + SPAN].astype(F32), jnp.exp(tot - cs), 0
                    ).astype(BF16)
                    fresh = mm(decayed, b_t[:, at], NT)
                    if local is not None:
                        fresh = fresh + per_head(local, jnp.exp(tot)[:, :STATE], 0)
                    local = fresh
                    ahead = ahead + tot
        for b in range(nb):
            at = slice(b * SPAN, (b + 1) * SPAN)
            for h in range(HEADS):
                hs = slice(h * HEADDIM, (h + 1) * HEADDIM)
                both = []
                for side in range(2):
                    col = (strand * nb + b) * 8 + h
                    e = part(sides[side][2], strand, b)[h : h + 1] - sides[side][4][:, col : col + 1]
                    both.append((scores[side, b] * jnp.exp(jnp.minimum(e, 0.0))).astype(BF16))
                y = mm(
                    own_s[strand, hs, b * 2 * SPAN : (b + 1) * 2 * SPAN],
                    jnp.concatenate(both, axis=0),
                )
                for side in range(2):
                    here, far_grow = grown[side, b]
                    y = y + from_s[strand, side, hs, at] * far_grow[h : h + 1]
                    if near[side, b]:
                        y = y + near_s[strand, side, hs, at] * here[h : h + 1]
                y_s[strand, hs, at] = y

    for h in range(HEADS):
        hs = slice(h * HEADDIM, (h + 1) * HEADDIM)
        gain = gain_ref[hs, :]
        gain = jnp.concatenate([gain] * nb, axis=1)
        total = None
        for strand in range(2):
            at = strand * INNER + h * HEADDIM
            g = y_s[strand, hs, :] * gate_ref[at : at + HEADDIM, :]
            mean_sq = jnp.mean(g * g, axis=0, keepdims=True)
            out = (g * lax.rsqrt(mean_sq + EPSILON) * gain).astype(BF16).astype(F32)
            total = out if total is None else total + out
        comb_s[hs, :] = total.astype(BF16)

    comb_t = comb_s[...]
    comb = jnp.transpose(comb_t.astype(F32)).astype(BF16)
    layer = mm(comb, wout_ref[...]).astype(BF16)
    layer_out[...] = layer
    layer = layer.astype(F32)
    sigma = 0.5 + 0.5 * jnp.tanh(0.5 * layer)
    act_high, act_low = split_two(layer * sigma)
    head_t = headt_ref[...]
    logits = mm(head_t, act_high, NT) + mm(head_t, act_low, NT)
    classes = 5
    real = lax.broadcasted_iota(jnp.int32, (8, length), 0) < classes
    expo = jnp.where(real, jnp.exp(logits), 0.0)
    prob = expo / jnp.sum(expo, axis=0, keepdims=True)
    target = (sub8 == tok_ref[0:1, :]).astype(F32)
    masked = values_of(me) > 0.5
    grad_logits = jnp.where(masked & real, (prob - target) / masked_total, 0.0)
    high, low = split_two(grad_logits)
    both = jnp.concatenate([high.astype(F32), low.astype(F32)], axis=0)
    head2 = jnp.concatenate([head_t.astype(F32)] * 2, axis=0).astype(BF16)
    grad_act = mm(jnp.transpose(both).astype(BF16), head2)
    slope = sigma * (1.0 + layer * (1.0 - sigma))
    grad_layer = (grad_act * slope).astype(BF16)
    core = me % 2
    half = INNER // 2
    send_out[...] = mm(
        comb_s[pl.ds(pl.multiple_of((1 - core) * half, half), half), :], grad_layer
    ).astype(BF16)
    keep_out[...] = mm(
        comb_s[pl.ds(pl.multiple_of(core * half, half), half), :], grad_layer
    ).astype(BF16)


def swap(value, axis, k):
    return lax.ppermute(value, axis, [(i, i ^ k) for i in range(lax.axis_size(axis))])


def strides(n):
    out, stride = [], 2
    while stride < n:
        radix = 4 if n // stride >= 4 else 2
        out.append((stride, radix))
        stride *= radix
    return out


def row_of(stack, index):
    return lax.dynamic_index_in_dim(stack, index, 0, False)


def tree_sum(parts):
    parts = [p.astype(F32) for p in parts]
    while len(parts) > 1:
        parts = [a + b for a, b in zip(parts[::2], parts[1::2])]
    return parts[0].astype(BF16)


def sum_all(send, keep, n):
    core = lax.axis_index("seq") % 2
    mine = lax.axis_index("dp")
    rows, cols = keep.shape
    part = tree_sum([keep, swap(send, "seq", 1)]).reshape(4, rows // 4, cols)
    got = [swap(row_of(part, mine ^ k), "dp", k) for k in (1, 2, 3)]
    part = tree_sum([row_of(part, mine)] + got)
    for stride, radix in strides(n):
        got = [swap(part, "seq", k * stride) for k in range(1, radix)]
        part = tree_sum([part] + got)
    got = [part] + [swap(part, "dp", k) for k in (1, 2, 3)]
    part = jnp.stack(
        [
            jnp.where(mine == j, got[0], jnp.where(mine == j ^ 1, got[1], jnp.where(mine == j ^ 2, got[2], got[3])))
            for j in range(4)
        ]
    ).reshape(rows, cols)
    other = swap(part, "seq", 1)
    low = jnp.where(core == 0, part, other)
    high = jnp.where(core == 0, other, part)
    return jnp.concatenate([low, high], axis=0).astype(F32)


def per_device(
    n, tokens, mask_pos, replace_ids, token_embedding_matrix, entry_scale_vector,
    input_projection_weight, increment_coefficients, conv_w, conv_b, dt_bias, decay_rate,
    gain_out, w_out, w_head,
):
    length = tokens.shape[1]
    width = w_out.shape[1]
    nb = length // SPAN
    rows = 2 * nb * 8
    gathered = jnp.concatenate(
        [tokens.astype(F32), swap(tokens, "seq", 1).astype(F32)], axis=0
    )
    for stride, radix in strides(n):
        gathered = jnp.concatenate(
            [gathered] + [swap(gathered, "seq", k * stride) for k in range(1, radix)], axis=0
        )
    shape = jax.ShapeDtypeStruct
    weights = (
        token_embedding_matrix, entry_scale_vector[None], input_projection_weight,
        increment_coefficients.T, conv_w, conv_b, dt_bias, decay_rate, gain_out[None], w_head.T,
        tokens, mask_pos, replace_ids,
    )
    masks = mask_pos.shape[1]
    wide = -(-masks // 128) * 128
    tables = pl.pallas_call(
        tables_kernel,
        in_specs=[pl.BlockSpec(memory_space=pltpu.HBM)] * len(weights),
        scratch_shapes=[pltpu.VMEM(w.shape, w.dtype) for w in weights]
        + [pltpu.VMEM((1, wide), jnp.int32)] * 2
        + [pltpu.SemaphoreType.DMA((len(weights),))],
        out_shape=(
            pltpu.VMEM((2, 2 * CONVW, 16 * KW), BF16),
            pltpu.VMEM((2 * INNER, length), F32),
            pltpu.VMEM((2, 2, HEADS, 8), F32),
            pltpu.VMEM((2, 2, HEADS, 8), F32),
            pltpu.VMEM((INNER, 128), F32),
            pltpu.VMEM((8, width), BF16),
            pltpu.VMEM((n * nb, SPAN), F32),
        ),
        compiler_params=pltpu.CompilerParams(vmem_limit_bytes=32 << 20),
        cost_estimate=pl.CostEstimate(flops=20_000_000, bytes_accessed=3_000_000, transcendentals=10_000),
        name="tables",
    )(*[pltpu.with_memory_space_constraint(w, pltpu.HBM) for w in weights])
    slots = n + 1
    spots = n - 1 if n <= 16 else 1
    operands = (gathered, *tables, w_out)
    layer_out, send, keep = pl.pallas_call(
        functools.partial(layer_kernel, n, length, lax.axis_size("dp") * masks),
        out_shape=(
            shape((length, width), BF16),
            pltpu.VMEM((INNER // 2, width), BF16),
            pltpu.VMEM((INNER // 2, width), BF16),
        ),
        scratch_shapes=[
            pltpu.VMEM((n + 2, length), F32),
            pltpu.VMEM((slots, rows, SPAN), F32),
            pltpu.VMEM((slots, rows, SPAN), F32),
            pltpu.VMEM((slots, rows, SPAN), F32),
            pltpu.VMEM((slots, rows, SPAN), F32),
            pltpu.VMEM((2, INNER, 2 * length), BF16),
            pltpu.VMEM((2, 2, INNER, length), F32),
            pltpu.VMEM((2, 2, INNER, length), F32),
            pltpu.VMEM((2, INNER, spots * length), BF16),
            pltpu.VMEM((2, 2 * STATE, spots * length), BF16),
            pltpu.VMEM((2, INNER, 2 * STATE), F32),
            pltpu.VMEM((2, INNER, length), F32),
            pltpu.VMEM((INNER, length), BF16),
        ],
        compiler_params=pltpu.CompilerParams(vmem_limit_bytes=32 << 20),
        cost_estimate=pl.CostEstimate(flops=2_000_000_000, bytes_accessed=4_000_000, transcendentals=4_000_000),
        name="layer",
    )(*operands)
    return (layer_out[None], sum_all(send, keep, n))


def solution(mesh):
    in_specs = (P("dp", "seq"), P("dp", None), P("dp", None)) + (P(),) * 11
    out_specs = (P("dp", "seq", None), P())
    return jax.shard_map(
        functools.partial(per_device, mesh.shape["seq"]),
        mesh=mesh, in_specs=in_specs, out_specs=out_specs, check_vma=False,
    )
```

```python
import functools

import jax
import jax.numpy as jnp
from jax import lax
from jax.experimental import pallas as pl
from jax.experimental.pallas import tpu as pltpu
from jax.sharding import PartitionSpec as P

HEADS = 8
HEADDIM = 64
STATE = 64
SPAN = 128
KW = 4
INNER = 512
CONVW = 640
EPSILON = 1e-05
F32 = jnp.float32
BF16 = jnp.bfloat16
HIGH = lax.Precision.HIGHEST
NN = (((1,), (0,)), ((), ()))
NT = (((1,), (1,)), ((), ()))
TN = (((0,), (0,)), ((), ()))


def mm(a, b, dims=NN, precision=None):
    return lax.dot_general(a, b, dims, precision=precision, preferred_element_type=F32)


def split_two(value):
    high = value.astype(BF16)
    return high, (value - high.astype(F32)).astype(BF16)


def eye(rows, cols, dtype=F32):
    return (
        lax.broadcasted_iota(jnp.int32, (rows, cols), 0)
        == lax.broadcasted_iota(jnp.int32, (rows, cols), 1)
    ).astype(dtype)


def silu_half(half):
    return half + half * jnp.tanh(half)


def tables_kernel(*refs):
    count = 13
    sources, outs, buffers = refs[:count], refs[count : count + 7], refs[count + 7 : 2 * count + 7]
    pos_s, rep_s, sem = refs[2 * count + 7 :]
    copies = [
        pltpu.make_async_copy(source, buffer, sem.at[i])
        for i, (source, buffer) in enumerate(zip(sources, buffers))
    ]
    for copy in copies:
        copy.start()
    for copy in copies:
        copy.wait()
    (
        emb_ref, scale_ref, win_ref, inc_ref, cw_ref, cb_ref, dtb_ref, rate_ref, gain_ref, head_ref,
        tok_ref, pos_ref, rep_ref,
    ) = buffers
    conv_out, gate_out, step_out, decay_out, gain_out, head_out, val_out = outs

    masks, wide, blocks = pos_ref.shape[1], pos_s.shape[1], val_out.shape[0]
    pos_s[...] = jnp.full_like(pos_s, -1)
    rep_s[...] = jnp.zeros_like(rep_s)
    pos_s[:, :masks] = pos_ref[...]
    rep_s[:, :masks] = rep_ref[...]
    pos = pos_s[...]
    block_hit = lax.broadcasted_iota(jnp.int32, (blocks, wide), 0) == (pos >> 7)
    put = jnp.where(block_hit, (rep_s[...] + 1).astype(F32), 0.0).astype(BF16)
    lane_hit = (lax.broadcasted_iota(jnp.int32, (SPAN, wide), 0) == (pos & 127)) & (pos >= 0)
    val_out[...] = mm(put, lane_hit.astype(F32).astype(BF16), NT)
    length = tok_ref.shape[1]
    nb = length // SPAN
    first = lax.axis_index("seq") * nb
    val = jnp.concatenate([val_out[pl.ds(first + b, 1), :] for b in range(nb)], axis=1)
    ids = jnp.where(val > 0.5, val - 1.0, tok_ref[...].astype(F32))
    hot = (lax.broadcasted_iota(jnp.int32, (8, length), 0).astype(F32) == ids).astype(F32)
    hot = jnp.concatenate([hot, hot], axis=0).astype(BF16)
    emb = emb_ref[...].astype(F32)
    none = jnp.zeros((2, emb.shape[1]), F32)
    rows = jnp.concatenate(
        [emb, none, emb[3:4], emb[2:3], emb[1:2], emb[0:1], emb[4:6], none], axis=0
    )
    mean_sq = jnp.mean(rows * rows, axis=-1, keepdims=True)
    normed = (rows * lax.rsqrt(mean_sq + EPSILON) * scale_ref[...]).astype(BF16)
    projected = mm(normed, win_ref[...]).astype(BF16).astype(F32)
    raw_t = mm(inc_ref[...], normed, NT)
    dtb_t = mm(eye(HEADS, HEADS), dtb_ref[...], NT, HIGH)
    rate_t = mm(eye(HEADS, HEADS), rate_ref[...], NT, HIGH)
    gate = projected[:, :INNER] * 0.5
    gate_t = jnp.transpose(silu_half(gate))
    mixed = projected[:, INNER:]
    for strand in range(2):
        high, low = split_two(gate_t[:, strand * 8 : strand * 8 + 8])
        gate_out[strand * INNER : (strand + 1) * INNER, :] = mm(jnp.concatenate([high, low], axis=1), hot)
    for side in range(2):
        for strand in range(2):
            param = side ^ strand
            mine = mixed[strand * 8 : strand * 8 + 8]
            taps = [cw_ref[param, j : j + 1, :] * mine for j in range(KW)]
            taps[0] = taps[0] + cb_ref[param : param + 1, :]
            table = jnp.transpose(jnp.concatenate(taps, axis=0) * 0.5)
            high, low = split_two(table)
            conv_out[side, strand * CONVW : (strand + 1) * CONVW, :] = jnp.concatenate(
                [high, low], axis=1
            )
            step = jax.nn.softplus(
                raw_t[:, strand * 8 : strand * 8 + 8] + dtb_t[:, param : param + 1]
            )
            step_out[side, strand] = step
            decay_out[side, strand] = -step * rate_t[:, param : param + 1]
    gain_out[...] = jnp.transpose(jnp.broadcast_to(gain_ref[...], (128, INNER)))
    classes, width = head_ref.shape
    head_out[...] = jnp.concatenate(
        [head_ref[...].astype(F32), jnp.zeros((8 - classes, width), F32)], axis=0
    ).astype(BF16)


def pick(table, ids):
    total = jnp.zeros((table.shape[0], ids.shape[1]), F32)
    for entry in range(6):
        total = jnp.where(ids == entry, table[:, entry : entry + 1], total)
    return total


def layer_kernel(
    n, length, masked_total,
    tok_ref, conv_ref, gate_ref, step_ref, decay_ref, gain_ref, headt_ref, val_s, wout_ref,
    layer_out, send_out, keep_out,
    ids_s, step_s, log_s, cum_s, tot_s, own_s, from_s, near_s, far_s, farb_s, state_s, y_s, comb_s,
):
    me = lax.axis_index("seq")
    nb = length // SPAN
    unrolled = n <= 16
    rows = 2 * nb * 8

    def loop(count, body):
        if unrolled:
            for k in range(count):
                body(k)
        else:
            pl.loop(0, count)(body)

    nothing = jnp.full((1, length), -1.0, F32)
    ids_s[0:1, :] = nothing
    ids_s[n + 1 : n + 2, :] = nothing

    def values_of(unit):
        return jnp.concatenate(
            [val_s[pl.ds(unit * nb + b, 1), :] for b in range(nb)], axis=1
        )

    def place(k):
        unit = me ^ k
        put_here = values_of(unit)
        own = tok_ref[pl.ds(k, 1), :]
        ids_s[pl.ds(unit + 1, 1), :] = jnp.where(put_here > 0.5, put_here - 1.0, own)

    loop(n, place)

    lane = lax.broadcasted_iota(jnp.int32, (1, length), 1)
    sub8 = lax.broadcasted_iota(jnp.int32, (8, length), 0).astype(F32)

    def one_hots(unit, side):
        here = ids_s[pl.ds(unit + 1, 1), :]
        beside = ids_s[pl.ds(unit + 2 * side, 1), :]
        out = [(sub8 == here).astype(F32)]
        for j in range(1, KW):
            if isinstance(side, int):
                shift = j if side == 0 else length - j
                border = (lane < j) if side == 0 else (lane >= length - j)
            else:
                shift = jnp.where(side == 0, j, length - j)
                border = jnp.where(side == 0, lane, length - 1 - lane) < j
            moved = jnp.where(
                border, pltpu.roll(beside, shift, 1), pltpu.roll(here, shift, 1)
            )
            out.append((sub8 == moved).astype(F32))
        hot = jnp.concatenate(out, axis=0).astype(BF16)
        return jnp.concatenate([hot, hot], axis=0)

    def slot_of(k):
        before = k < me
        unit = jnp.where(before, me - 1 - k, k + 1)
        side = jnp.where(before, 0, 1)
        return unit, side

    def fill(slot, unit, side):
        here = ids_s[pl.ds(unit + 1, 1), :]
        for source, target in ((step_ref, step_s), (decay_ref, log_s)):
            parts = []
            for strand in range(2):
                full = pick(source[side, strand], here)
                parts += [full[:, b * SPAN : (b + 1) * SPAN] for b in range(nb)]
            target[slot] = jnp.concatenate(parts, axis=0)

    def fill_other(k):
        unit, side = slot_of(k)
        fill(k, unit, side)

    loop(n - 1, fill_other)
    fill(n - 1, me, 0)
    fill(n, me, 1)
    logs = log_s[...].reshape((n + 1) * rows, SPAN)
    before = (
        lax.broadcasted_iota(jnp.int32, (SPAN, SPAN), 0)
        <= lax.broadcasted_iota(jnp.int32, (SPAN, SPAN), 1)
    ).astype(F32)
    cum = mm(logs, before, NN, HIGH).reshape(n + 1, rows, SPAN)
    cum_s[...] = cum
    tot_s[...] = jnp.broadcast_to(cum[:, :, SPAN - 1 :], cum.shape)

    def part(array, strand, b):
        start = (strand * nb + b) * 8
        return array[start : start + 8]

    def weigh(k, far):
        side_back = k >= me
        far = [jnp.where(k == me, 0.0, value) for value in far]
        steps, cums, logs_k, tots = step_s[k], cum_s[k], log_s[k], tot_s[k]
        new = []
        parts = [None] * (2 * nb)
        for strand in range(2):
            whole = sum(part(tots, strand, b) for b in range(nb))
            ahead = jnp.zeros((8, SPAN), F32)
            for b in range(nb):
                behind = whole - ahead - part(tots, strand, b)
                e_fwd = part(tots, strand, b) - part(cums, strand, b) + behind
                e_bwd = part(cums, strand, b) - part(logs_k, strand, b) + ahead
                e = jnp.where(side_back, e_bwd, e_fwd) + far[strand]
                parts[strand * nb + b] = part(steps, strand, b) * jnp.exp(e)
                ahead = ahead + part(tots, strand, b)
            new.append(far[strand] + whole)
        step_s[k] = jnp.concatenate(parts, axis=0)
        return new

    far = [jnp.zeros((8, SPAN), F32)] * 2
    if unrolled:
        for k in range(n - 1):
            far = weigh(k, far)
    else:
        lax.fori_loop(0, n - 1, lambda k, c: tuple(weigh(k, list(c))), tuple(far))

    def across(array, strand):
        return jnp.concatenate([part(array, strand, b) for b in range(nb)], axis=1)

    def per_head(x, row8, first):
        return jnp.concatenate(
            [
                x[h * HEADDIM : (h + 1) * HEADDIM] * row8[first + h : first + h + 1]
                for h in range(x.shape[0] // HEADDIM)
            ],
            axis=0,
        )

    def gather_state(k, spot):
        unit, side = slot_of(k)
        hot = one_hots(unit, side)
        weight = step_s[k]
        at = slice(spot * length, (spot + 1) * length)
        for strand in range(2):
            row8 = across(weight, strand)
            base = strand * CONVW
            half = mm(conv_ref[side, base : base + INNER, :], hot).astype(BF16)
            far_s[strand, :, at] = per_head(silu_half(half), row8.astype(BF16), 0)
            b_t = silu_half(mm(conv_ref[side, base + INNER : base + INNER + STATE, :], hot))
            farb_s[strand, :STATE, at] = jnp.where(side == 0, b_t, 0.0).astype(BF16)
            farb_s[strand, STATE:, at] = jnp.where(side == 0, 0.0, b_t).astype(BF16)

    if unrolled:
        for k in range(n - 1):
            gather_state(k, k)
        for strand in range(2):
            state_s[strand] = mm(far_s[strand], farb_s[strand], NT)
    else:
        state_s[...] = jnp.zeros_like(state_s)

        def add_state(k):
            gather_state(k, 0)
            for strand in range(2):
                state_s[strand] += mm(far_s[strand], farb_s[strand], NT)

        loop(n - 1, add_state)

    row_i = lax.broadcasted_iota(jnp.int32, (SPAN, SPAN), 0)
    col_i = lax.broadcasted_iota(jnp.int32, (SPAN, SPAN), 1)
    sides = []
    for side in range(2):
        slot = n - 1 + side
        steps, cums, logs_k, tots = step_s[slot], cum_s[slot], log_s[slot], tot_s[slot]
        if side == 1:
            cums = tots - cums + logs_k
        sides.append((one_hots(me, side), steps, cums, tots, jnp.transpose(cums)))
    for strand in range(2):
        base = strand * CONVW
        states = state_s[strand].astype(BF16)
        scores, grown, near = {}, {}, {}
        for side in range(2):
            hot, steps, cums, tots, _ = sides[side]
            row8 = across(steps, strand)
            for c in range(4):
                half = mm(conv_ref[side, base + c * 128 : base + (c + 1) * 128, :], hot).astype(BF16)
                x = per_head(silu_half(half), row8.astype(BF16), 2 * c)
                for b in range(nb):
                    to = (b * 2 + side) * SPAN
                    own_s[strand, c * 128 : (c + 1) * 128, to : to + SPAN] = x[:, b * SPAN : (b + 1) * SPAN]
            bc_t = silu_half(mm(conv_ref[side, base + INNER : base + CONVW, :], hot))
            c_only = bc_t[STATE:]
            none = jnp.zeros_like(c_only)
            c_both = jnp.concatenate([c_only, none] if side == 0 else [none, c_only], axis=0)
            from_s[strand, side] = mm(states, c_both.astype(BF16))
            c_t, b_t = c_only.astype(BF16), bc_t[:STATE].astype(BF16)
            ahead = jnp.zeros((8, SPAN), F32)
            local = None
            for step_index in range(nb):
                b = step_index if side == 0 else nb - 1 - step_index
                at = slice(b * SPAN, (b + 1) * SPAN)
                b_rows = jnp.transpose(bc_t[:, at])[:, :STATE].astype(BF16)
                causal = (row_i <= col_i) if side == 0 else (row_i >= col_i)
                scores[side, b] = jnp.where(causal, mm(b_rows, c_t[:, at]), 0.0)
                cs, tot = part(cums, strand, b), part(tots, strand, b)
                grown[side, b] = (jnp.exp(cs), jnp.exp(cs + ahead))
                near[side, b] = local is not None
                if local is not None:
                    near_s[strand, side, :, at] = mm(local.astype(BF16), c_t[:, at])
                if step_index < nb - 1:
                    to = (b * 2 + side) * SPAN
                    decayed = per_head(
                        own_s[strand, :, to : to + SPAN].astype(F32), jnp.exp(tot - cs), 0
                    ).astype(BF16)
                    fresh = mm(decayed, b_t[:, at], NT)
                    if local is not None:
                        fresh = fresh + per_head(local, jnp.exp(tot)[:, :STATE], 0)
                    local = fresh
                    ahead = ahead + tot
        for b in range(nb):
            at = slice(b * SPAN, (b + 1) * SPAN)
            for h in range(HEADS):
                hs = slice(h * HEADDIM, (h + 1) * HEADDIM)
                both = []
                for side in range(2):
                    col = (strand * nb + b) * 8 + h
                    e = part(sides[side][2], strand, b)[h : h + 1] - sides[side][4][:, col : col + 1]
                    both.append((scores[side, b] * jnp.exp(jnp.minimum(e, 0.0))).astype(BF16))
                y = mm(
                    own_s[strand, hs, b * 2 * SPAN : (b + 1) * 2 * SPAN],
                    jnp.concatenate(both, axis=0),
                )
                for side in range(2):
                    here, far_grow = grown[side, b]
                    y = y + from_s[strand, side, hs, at] * far_grow[h : h + 1]
                    if near[side, b]:
                        y = y + near_s[strand, side, hs, at] * here[h : h + 1]
                y_s[strand, hs, at] = y

    for h in range(HEADS):
        hs = slice(h * HEADDIM, (h + 1) * HEADDIM)
        gain = gain_ref[hs, :]
        gain = jnp.concatenate([gain] * nb, axis=1)
        total = None
        for strand in range(2):
            at = strand * INNER + h * HEADDIM
            g = y_s[strand, hs, :] * gate_ref[at : at + HEADDIM, :]
            mean_sq = jnp.mean(g * g, axis=0, keepdims=True)
            out = (g * lax.rsqrt(mean_sq + EPSILON) * gain).astype(BF16).astype(F32)
            total = out if total is None else total + out
        comb_s[hs, :] = total.astype(BF16)

    comb_t = comb_s[...]
    comb = jnp.transpose(comb_t.astype(F32)).astype(BF16)
    layer = mm(comb, wout_ref[...]).astype(BF16)
    layer_out[...] = layer
    layer = layer.astype(F32)
    sigma = 0.5 + 0.5 * jnp.tanh(0.5 * layer)
    act_high, act_low = split_two(layer * sigma)
    head_t = headt_ref[...]
    logits = mm(head_t, act_high, NT) + mm(head_t, act_low, NT)
    classes = 5
    real = lax.broadcasted_iota(jnp.int32, (8, length), 0) < classes
    expo = jnp.where(real, jnp.exp(logits), 0.0)
    prob = expo / jnp.sum(expo, axis=0, keepdims=True)
    target = (sub8 == tok_ref[0:1, :]).astype(F32)
    masked = values_of(me) > 0.5
    grad_logits = jnp.where(masked & real, (prob - target) / masked_total, 0.0)
    high, low = split_two(grad_logits)
    both = jnp.concatenate([high.astype(F32), low.astype(F32)], axis=0)
    head2 = jnp.concatenate([head_t.astype(F32)] * 2, axis=0).astype(BF16)
    grad_act = mm(jnp.transpose(both).astype(BF16), head2)
    slope = sigma * (1.0 + layer * (1.0 - sigma))
    grad_layer = (grad_act * slope).astype(BF16)
    core = me % 2
    half = INNER // 2
    send_out[...] = mm(
        comb_s[pl.ds(pl.multiple_of((1 - core) * half, half), half), :], grad_layer
    ).astype(BF16)
    keep_out[...] = mm(
        comb_s[pl.ds(pl.multiple_of(core * half, half), half), :], grad_layer
    ).astype(BF16)


def swap(value, axis, k):
    return lax.ppermute(value, axis, [(i, i ^ k) for i in range(lax.axis_size(axis))])


def strides(n):
    out, stride = [], 2
    while stride < n:
        radix = 4 if n // stride >= 4 else 2
        out.append((stride, radix))
        stride *= radix
    return out


def row_of(stack, index):
    return lax.dynamic_index_in_dim(stack, index, 0, False)


def tree_sum(parts):
    parts = [p.astype(F32) for p in parts]
    while len(parts) > 1:
        parts = [a + b for a, b in zip(parts[::2], parts[1::2])]
    return parts[0].astype(BF16)


def sum_all(send, keep, n):
    core = lax.axis_index("seq") % 2
    mine = lax.axis_index("dp")
    rows, cols = keep.shape
    part = tree_sum([keep, swap(send, "seq", 1)]).reshape(4, rows // 4, cols)
    got = [swap(row_of(part, mine ^ k), "dp", k) for k in (1, 2, 3)]
    part = tree_sum([row_of(part, mine)] + got)
    for stride, radix in strides(n):
        got = [swap(part, "seq", k * stride) for k in range(1, radix)]
        part = tree_sum([part] + got)
    got = [part] + [swap(part, "dp", k) for k in (1, 2, 3)]
    part = jnp.stack(
        [
            jnp.where(mine == j, got[0], jnp.where(mine == j ^ 1, got[1], jnp.where(mine == j ^ 2, got[2], got[3])))
            for j in range(4)
        ]
    ).reshape(rows, cols)
    other = swap(part, "seq", 1)
    low = jnp.where(core == 0, part, other)
    high = jnp.where(core == 0, other, part)
    return jnp.concatenate([low, high], axis=0).astype(F32)


def per_device(
    n, tokens, mask_pos, replace_ids, token_embedding_matrix, entry_scale_vector,
    input_projection_weight, increment_coefficients, conv_w, conv_b, dt_bias, decay_rate,
    gain_out, w_out, w_head,
):
    length = tokens.shape[1]
    width = w_out.shape[1]
    nb = length // SPAN
    rows = 2 * nb * 8
    gathered = jnp.concatenate(
        [tokens.astype(F32), swap(tokens, "seq", 1).astype(F32)], axis=0
    )
    for stride, radix in strides(n):
        gathered = jnp.concatenate(
            [gathered] + [swap(gathered, "seq", k * stride) for k in range(1, radix)], axis=0
        )
    shape = jax.ShapeDtypeStruct
    weights = (
        token_embedding_matrix, entry_scale_vector[None], input_projection_weight,
        increment_coefficients.T, conv_w, conv_b, dt_bias, decay_rate, gain_out[None], w_head.T,
        tokens, mask_pos, replace_ids,
    )
    masks = mask_pos.shape[1]
    wide = -(-masks // 128) * 128
    tables = pl.pallas_call(
        tables_kernel,
        in_specs=[pl.BlockSpec(memory_space=pltpu.HBM)] * len(weights),
        scratch_shapes=[pltpu.VMEM(w.shape, w.dtype) for w in weights]
        + [pltpu.VMEM((1, wide), jnp.int32)] * 2
        + [pltpu.SemaphoreType.DMA((len(weights),))],
        out_shape=(
            pltpu.VMEM((2, 2 * CONVW, 16 * KW), BF16),
            pltpu.VMEM((2 * INNER, length), F32),
            pltpu.VMEM((2, 2, HEADS, 8), F32),
            pltpu.VMEM((2, 2, HEADS, 8), F32),
            pltpu.VMEM((INNER, 128), F32),
            pltpu.VMEM((8, width), BF16),
            pltpu.VMEM((n * nb, SPAN), F32),
        ),
        compiler_params=pltpu.CompilerParams(vmem_limit_bytes=32 << 20),
        cost_estimate=pl.CostEstimate(flops=20_000_000, bytes_accessed=3_000_000, transcendentals=10_000),
        name="tables",
    )(*[pltpu.with_memory_space_constraint(w, pltpu.HBM) for w in weights])
    slots = n + 1
    spots = n - 1 if n <= 16 else 1
    operands = (gathered, *tables, w_out)
    layer_out, send, keep = pl.pallas_call(
        functools.partial(layer_kernel, n, length, lax.axis_size("dp") * masks),
        out_shape=(
            shape((length, width), BF16),
            pltpu.VMEM((INNER // 2, width), BF16),
            pltpu.VMEM((INNER // 2, width), BF16),
        ),
        scratch_shapes=[
            pltpu.VMEM((n + 2, length), F32),
            pltpu.VMEM((slots, rows, SPAN), F32),
            pltpu.VMEM((slots, rows, SPAN), F32),
            pltpu.VMEM((slots, rows, SPAN), F32),
            pltpu.VMEM((slots, rows, SPAN), F32),
            pltpu.VMEM((2, INNER, 2 * length), BF16),
            pltpu.VMEM((2, 2, INNER, length), F32),
            pltpu.VMEM((2, 2, INNER, length), F32),
            pltpu.VMEM((2, INNER, spots * length), BF16),
            pltpu.VMEM((2, 2 * STATE, spots * length), BF16),
            pltpu.VMEM((2, INNER, 2 * STATE), F32),
            pltpu.VMEM((2, INNER, length), F32),
            pltpu.VMEM((INNER, length), BF16),
        ],
        compiler_params=pltpu.CompilerParams(vmem_limit_bytes=32 << 20),
        cost_estimate=pl.CostEstimate(flops=2_000_000_000, bytes_accessed=4_000_000, transcendentals=4_000_000),
        name="layer",
    )(*operands)
    return (layer_out[None], sum_all(send, keep, n))


def solution(mesh):
    in_specs = (P("dp", "seq"), P("dp", None), P("dp", None)) + (P(),) * 11
    out_specs = (P("dp", "seq", None), P())
    return jax.shard_map(
        functools.partial(per_device, mesh.shape["seq"]),
        mesh=mesh, in_specs=in_specs, out_specs=out_specs, check_vma=False,
    )
```

```python
import functools

import jax
import jax.numpy as jnp
from jax import lax
from jax.experimental import pallas as pl
from jax.experimental.pallas import tpu as pltpu
from jax.sharding import PartitionSpec as P

HEADS = 8
HEADDIM = 64
STATE = 64
SPAN = 128
KW = 4
INNER = 512
CONVW = 640
EPSILON = 1e-05
F32 = jnp.float32
BF16 = jnp.bfloat16
HIGH = lax.Precision.HIGHEST
NN = (((1,), (0,)), ((), ()))
NT = (((1,), (1,)), ((), ()))
TN = (((0,), (0,)), ((), ()))


def mm(a, b, dims=NN, precision=None):
    return lax.dot_general(a, b, dims, precision=precision, preferred_element_type=F32)


def split_two(value):
    high = value.astype(BF16)
    return high, (value - high.astype(F32)).astype(BF16)


def eye(rows, cols, dtype=F32):
    return (
        lax.broadcasted_iota(jnp.int32, (rows, cols), 0)
        == lax.broadcasted_iota(jnp.int32, (rows, cols), 1)
    ).astype(dtype)


def silu_half(half):
    return half + half * jnp.tanh(half)


def tables_kernel(*refs):
    count = 13
    sources, outs, buffers = refs[:count], refs[count : count + 7], refs[count + 7 : 2 * count + 7]
    pos_s, rep_s, sem = refs[2 * count + 7 :]
    copies = [
        pltpu.make_async_copy(source, buffer, sem.at[i])
        for i, (source, buffer) in enumerate(zip(sources, buffers))
    ]
    for copy in copies:
        copy.start()
    for copy in copies:
        copy.wait()
    (
        emb_ref, scale_ref, win_ref, inc_ref, cw_ref, cb_ref, dtb_ref, rate_ref, gain_ref, head_ref,
        tok_ref, pos_ref, rep_ref,
    ) = buffers
    conv_out, gate_out, step_out, decay_out, gain_out, head_out, val_out = outs

    masks, wide, blocks = pos_ref.shape[1], pos_s.shape[1], val_out.shape[0]
    pos_s[...] = jnp.full_like(pos_s, -1)
    rep_s[...] = jnp.zeros_like(rep_s)
    pos_s[:, :masks] = pos_ref[...]
    rep_s[:, :masks] = rep_ref[...]
    pos = pos_s[...]
    block_hit = lax.broadcasted_iota(jnp.int32, (blocks, wide), 0) == (pos >> 7)
    put = jnp.where(block_hit, (rep_s[...] + 1).astype(F32), 0.0).astype(BF16)
    lane_hit = (lax.broadcasted_iota(jnp.int32, (SPAN, wide), 0) == (pos & 127)) & (pos >= 0)
    val_out[...] = mm(put, lane_hit.astype(F32).astype(BF16), NT)
    length = tok_ref.shape[1]
    nb = length // SPAN
    first = lax.axis_index("seq") * nb
    val = jnp.concatenate([val_out[pl.ds(first + b, 1), :] for b in range(nb)], axis=1)
    ids = jnp.where(val > 0.5, val - 1.0, tok_ref[...].astype(F32))
    hot = (lax.broadcasted_iota(jnp.int32, (8, length), 0).astype(F32) == ids).astype(F32)
    hot = jnp.concatenate([hot, hot], axis=0).astype(BF16)
    emb = emb_ref[...].astype(F32)
    none = jnp.zeros((2, emb.shape[1]), F32)
    rows = jnp.concatenate(
        [emb, none, emb[3:4], emb[2:3], emb[1:2], emb[0:1], emb[4:6], none], axis=0
    )
    mean_sq = jnp.mean(rows * rows, axis=-1, keepdims=True)
    normed = (rows * lax.rsqrt(mean_sq + EPSILON) * scale_ref[...]).astype(BF16)
    projected = mm(normed, win_ref[...]).astype(BF16).astype(F32)
    raw_t = mm(inc_ref[...], normed, NT)
    dtb_t = mm(eye(HEADS, HEADS), dtb_ref[...], NT, HIGH)
    rate_t = mm(eye(HEADS, HEADS), rate_ref[...], NT, HIGH)
    gate = projected[:, :INNER] * 0.5
    gate_t = jnp.transpose(silu_half(gate))
    mixed = projected[:, INNER:]
    for strand in range(2):
        high, low = split_two(gate_t[:, strand * 8 : strand * 8 + 8])
        gate_out[strand * INNER : (strand + 1) * INNER, :] = mm(jnp.concatenate([high, low], axis=1), hot)
    for side in range(2):
        for strand in range(2):
            param = side ^ strand
            mine = mixed[strand * 8 : strand * 8 + 8]
            taps = [cw_ref[param, j : j + 1, :] * mine for j in range(KW)]
            taps[0] = taps[0] + cb_ref[param : param + 1, :]
            table = jnp.transpose(jnp.concatenate(taps, axis=0) * 0.5)
            high, low = split_two(table)
            conv_out[side, strand * CONVW : (strand + 1) * CONVW, :] = jnp.concatenate(
                [high, low], axis=1
            )
            step = jax.nn.softplus(
                raw_t[:, strand * 8 : strand * 8 + 8] + dtb_t[:, param : param + 1]
            )
            step_out[side, strand] = step
            decay_out[side, strand] = -step * rate_t[:, param : param + 1]
    gain_out[...] = jnp.transpose(jnp.broadcast_to(gain_ref[...], (128, INNER)))
    classes, width = head_ref.shape
    head_out[...] = jnp.concatenate(
        [head_ref[...].astype(F32), jnp.zeros((8 - classes, width), F32)], axis=0
    ).astype(BF16)


def pick(table, ids):
    total = jnp.zeros((table.shape[0], ids.shape[1]), F32)
    for entry in range(6):
        total = jnp.where(ids == entry, table[:, entry : entry + 1], total)
    return total


def layer_kernel(
    n, length, masked_total,
    tok_ref, conv_ref, gate_ref, step_ref, decay_ref, gain_ref, headt_ref, val_s, wout_ref,
    layer_hbm, send_out, keep_out, layer_out, sem,
    ids_s, step_s, log_s, cum_s, tot_s, own_s, from_s, near_s, far_s, farb_s, state_s, y_s, comb_s,
):
    me = lax.axis_index("seq")
    nb = length // SPAN
    unrolled = n <= 16
    rows = 2 * nb * 8

    def loop(count, body):
        if unrolled:
            for k in range(count):
                body(k)
        else:
            pl.loop(0, count)(body)

    nothing = jnp.full((1, length), -1.0, F32)
    ids_s[0:1, :] = nothing
    ids_s[n + 1 : n + 2, :] = nothing

    def values_of(unit):
        return jnp.concatenate(
            [val_s[pl.ds(unit * nb + b, 1), :] for b in range(nb)], axis=1
        )

    def place(k):
        unit = me ^ k
        put_here = values_of(unit)
        own = tok_ref[pl.ds(k, 1), :]
        ids_s[pl.ds(unit + 1, 1), :] = jnp.where(put_here > 0.5, put_here - 1.0, own)

    loop(n, place)

    lane = lax.broadcasted_iota(jnp.int32, (1, length), 1)
    sub8 = lax.broadcasted_iota(jnp.int32, (8, length), 0).astype(F32)

    def one_hots(unit, side):
        here = ids_s[pl.ds(unit + 1, 1), :]
        beside = ids_s[pl.ds(unit + 2 * side, 1), :]
        out = [(sub8 == here).astype(F32)]
        for j in range(1, KW):
            if isinstance(side, int):
                shift = j if side == 0 else length - j
                border = (lane < j) if side == 0 else (lane >= length - j)
            else:
                shift = jnp.where(side == 0, j, length - j)
                border = jnp.where(side == 0, lane, length - 1 - lane) < j
            moved = jnp.where(
                border, pltpu.roll(beside, shift, 1), pltpu.roll(here, shift, 1)
            )
            out.append((sub8 == moved).astype(F32))
        hot = jnp.concatenate(out, axis=0).astype(BF16)
        return jnp.concatenate([hot, hot], axis=0)

    def slot_of(k):
        before = k < me
        unit = jnp.where(before, me - 1 - k, k + 1)
        side = jnp.where(before, 0, 1)
        return unit, side

    def fill(slot, unit, side):
        here = ids_s[pl.ds(unit + 1, 1), :]
        for source, target in ((step_ref, step_s), (decay_ref, log_s)):
            parts = []
            for strand in range(2):
                full = pick(source[side, strand], here)
                parts += [full[:, b * SPAN : (b + 1) * SPAN] for b in range(nb)]
            target[slot] = jnp.concatenate(parts, axis=0)

    def fill_other(k):
        unit, side = slot_of(k)
        fill(k, unit, side)

    loop(n - 1, fill_other)
    fill(n - 1, me, 0)
    fill(n, me, 1)
    logs = log_s[...].reshape((n + 1) * rows, SPAN)
    before = (
        lax.broadcasted_iota(jnp.int32, (SPAN, SPAN), 0)
        <= lax.broadcasted_iota(jnp.int32, (SPAN, SPAN), 1)
    ).astype(F32)
    cum = mm(logs, before, NN, HIGH).reshape(n + 1, rows, SPAN)
    cum_s[...] = cum
    tot_s[...] = jnp.broadcast_to(cum[:, :, SPAN - 1 :], cum.shape)

    def part(array, strand, b):
        start = (strand * nb + b) * 8
        return array[start : start + 8]

    def weigh(k, far):
        side_back = k >= me
        far = [jnp.where(k == me, 0.0, value) for value in far]
        steps, cums, logs_k, tots = step_s[k], cum_s[k], log_s[k], tot_s[k]
        new = []
        parts = [None] * (2 * nb)
        for strand in range(2):
            whole = sum(part(tots, strand, b) for b in range(nb))
            ahead = jnp.zeros((8, SPAN), F32)
            for b in range(nb):
                behind = whole - ahead - part(tots, strand, b)
                e_fwd = part(tots, strand, b) - part(cums, strand, b) + behind
                e_bwd = part(cums, strand, b) - part(logs_k, strand, b) + ahead
                e = jnp.where(side_back, e_bwd, e_fwd) + far[strand]
                parts[strand * nb + b] = part(steps, strand, b) * jnp.exp(e)
                ahead = ahead + part(tots, strand, b)
            new.append(far[strand] + whole)
        step_s[k] = jnp.concatenate(parts, axis=0)
        return new

    far = [jnp.zeros((8, SPAN), F32)] * 2
    if unrolled:
        for k in range(n - 1):
            far = weigh(k, far)
    else:
        lax.fori_loop(0, n - 1, lambda k, c: tuple(weigh(k, list(c))), tuple(far))

    def across(array, strand):
        return jnp.concatenate([part(array, strand, b) for b in range(nb)], axis=1)

    def per_head(x, row8, first):
        return jnp.concatenate(
            [
                x[h * HEADDIM : (h + 1) * HEADDIM] * row8[first + h : first + h + 1]
                for h in range(x.shape[0] // HEADDIM)
            ],
            axis=0,
        )

    def gather_state(k, spot):
        unit, side = slot_of(k)
        hot = one_hots(unit, side)
        weight = step_s[k]
        at = slice(spot * length, (spot + 1) * length)
        for strand in range(2):
            row8 = across(weight, strand)
            base = strand * CONVW
            for c in range(4):
                half = mm(conv_ref[side, base + c * 128 : base + (c + 1) * 128, :], hot).astype(BF16)
                far_s[strand, c * 128 : (c + 1) * 128, at] = per_head(
                    silu_half(half), row8.astype(BF16), 2 * c
                )
            b_t = silu_half(mm(conv_ref[side, base + INNER : base + INNER + STATE, :], hot))
            farb_s[strand, :STATE, at] = jnp.where(side == 0, b_t, 0.0).astype(BF16)
            farb_s[strand, STATE:, at] = jnp.where(side == 0, 0.0, b_t).astype(BF16)

    if unrolled:
        for k in range(n - 1):
            gather_state(k, k)
        for strand in range(2):
            state_s[strand] = mm(far_s[strand], farb_s[strand], NT)
    else:
        state_s[...] = jnp.zeros_like(state_s)

        def add_state(k):
            gather_state(k, 0)
            for strand in range(2):
                state_s[strand] += mm(far_s[strand], farb_s[strand], NT)

        loop(n - 1, add_state)

    row_i = lax.broadcasted_iota(jnp.int32, (SPAN, SPAN), 0)
    col_i = lax.broadcasted_iota(jnp.int32, (SPAN, SPAN), 1)
    sides = []
    for side in range(2):
        slot = n - 1 + side
        steps, cums, logs_k, tots = step_s[slot], cum_s[slot], log_s[slot], tot_s[slot]
        if side == 1:
            cums = tots - cums + logs_k
        sides.append((one_hots(me, side), steps, cums, tots, jnp.transpose(cums)))
    for strand in range(2):
        base = strand * CONVW
        states = state_s[strand].astype(BF16)
        scores, grown, near = {}, {}, {}
        for side in range(2):
            hot, steps, cums, tots, _ = sides[side]
            row8 = across(steps, strand)
            for c in range(4):
                half = mm(conv_ref[side, base + c * 128 : base + (c + 1) * 128, :], hot)
                x = per_head(silu_half(half), row8, 2 * c).astype(BF16)
                for b in range(nb):
                    to = (b * 2 + side) * SPAN
                    own_s[strand, c * 128 : (c + 1) * 128, to : to + SPAN] = x[:, b * SPAN : (b + 1) * SPAN]
            bc_t = silu_half(mm(conv_ref[side, base + INNER : base + CONVW, :], hot))
            c_only = bc_t[STATE:]
            none = jnp.zeros_like(c_only)
            c_both = jnp.concatenate([c_only, none] if side == 0 else [none, c_only], axis=0)
            from_s[strand, side] = mm(states, c_both.astype(BF16))
            c_t, b_t = c_only.astype(BF16), bc_t[:STATE].astype(BF16)
            ahead = jnp.zeros((8, SPAN), F32)
            local = None
            for step_index in range(nb):
                b = step_index if side == 0 else nb - 1 - step_index
                at = slice(b * SPAN, (b + 1) * SPAN)
                b_rows = jnp.transpose(bc_t[:, at])[:, :STATE].astype(BF16)
                causal = (row_i <= col_i) if side == 0 else (row_i >= col_i)
                scores[side, b] = jnp.where(causal, mm(b_rows, c_t[:, at]), 0.0)
                cs, tot = part(cums, strand, b), part(tots, strand, b)
                grown[side, b] = (jnp.exp(cs), jnp.exp(cs + ahead))
                near[side, b] = local is not None
                if local is not None:
                    near_s[strand, side, :, at] = mm(local.astype(BF16), c_t[:, at])
                if step_index < nb - 1:
                    to = (b * 2 + side) * SPAN
                    decayed = per_head(
                        own_s[strand, :, to : to + SPAN].astype(F32), jnp.exp(tot - cs), 0
                    ).astype(BF16)
                    fresh = mm(decayed, b_t[:, at], NT)
                    if local is not None:
                        fresh = fresh + per_head(local, jnp.exp(tot)[:, :STATE], 0)
                    local = fresh
                    ahead = ahead + tot
        for b in range(nb):
            at = slice(b * SPAN, (b + 1) * SPAN)
            for h in range(HEADS):
                hs = slice(h * HEADDIM, (h + 1) * HEADDIM)
                both = []
                for side in range(2):
                    col = (strand * nb + b) * 8 + h
                    e = part(sides[side][2], strand, b)[h : h + 1] - sides[side][4][:, col : col + 1]
                    both.append((scores[side, b] * jnp.exp(jnp.minimum(e, 0.0))).astype(BF16))
                y = mm(
                    own_s[strand, hs, b * 2 * SPAN : (b + 1) * 2 * SPAN],
                    jnp.concatenate(both, axis=0),
                )
                for side in range(2):
                    here, far_grow = grown[side, b]
                    y = y + from_s[strand, side, hs, at] * far_grow[h : h + 1]
                    if near[side, b]:
                        y = y + near_s[strand, side, hs, at] * here[h : h + 1]
                y_s[strand, hs, at] = y

    for h in range(HEADS):
        hs = slice(h * HEADDIM, (h + 1) * HEADDIM)
        gain = gain_ref[hs, :]
        gain = jnp.concatenate([gain] * nb, axis=1)
        total = None
        for strand in range(2):
            at = strand * INNER + h * HEADDIM
            g = y_s[strand, hs, :] * gate_ref[at : at + HEADDIM, :]
            mean_sq = jnp.mean(g * g, axis=0, keepdims=True)
            out = (g * lax.rsqrt(mean_sq + EPSILON) * gain).astype(BF16).astype(F32)
            total = out if total is None else total + out
        comb_s[hs, :] = total.astype(BF16)

    comb_t = comb_s[...]
    comb = jnp.transpose(comb_t.astype(F32)).astype(BF16)
    layer = mm(comb, wout_ref[...]).astype(BF16)
    layer_out[...] = layer
    write = pltpu.make_async_copy(layer_out, layer_hbm, sem)
    write.start()
    layer = layer.astype(F32)
    sigma = 0.5 + 0.5 * jnp.tanh(0.5 * layer)
    act_high, act_low = split_two(layer * sigma)
    head_t = headt_ref[...]
    logits = mm(head_t, act_high, NT) + mm(head_t, act_low, NT)
    classes = 5
    real = lax.broadcasted_iota(jnp.int32, (8, length), 0) < classes
    expo = jnp.where(real, jnp.exp(logits), 0.0)
    prob = expo / jnp.sum(expo, axis=0, keepdims=True)
    target = (sub8 == tok_ref[0:1, :]).astype(F32)
    masked = values_of(me) > 0.5
    grad_logits = jnp.where(masked & real, (prob - target) / masked_total, 0.0)
    high, low = split_two(grad_logits)
    both = jnp.concatenate([high.astype(F32), low.astype(F32)], axis=0)
    head2 = jnp.concatenate([head_t.astype(F32)] * 2, axis=0).astype(BF16)
    grad_act = mm(jnp.transpose(both).astype(BF16), head2)
    slope = sigma * (1.0 + layer * (1.0 - sigma))
    grad_layer = (grad_act * slope).astype(BF16)
    core = me % 2
    half = INNER // 2
    send_out[...] = mm(
        comb_s[pl.ds(pl.multiple_of((1 - core) * half, half), half), :], grad_layer
    ).astype(BF16)
    keep_out[...] = mm(
        comb_s[pl.ds(pl.multiple_of(core * half, half), half), :], grad_layer
    ).astype(BF16)
    write.wait()


def swap(value, axis, k):
    return lax.ppermute(value, axis, [(i, i ^ k) for i in range(lax.axis_size(axis))])


def strides(n):
    out, stride = [], 2
    while stride < n:
        radix = 4 if n // stride >= 4 else 2
        out.append((stride, radix))
        stride *= radix
    return out


def row_of(stack, index):
    return lax.dynamic_index_in_dim(stack, index, 0, False)


def tree_sum(parts):
    parts = [p.astype(F32) for p in parts]
    while len(parts) > 1:
        parts = [a + b for a, b in zip(parts[::2], parts[1::2])]
    return parts[0].astype(BF16)


def sum_all(send, keep, n):
    core = lax.axis_index("seq") % 2
    mine = lax.axis_index("dp")
    rows, cols = keep.shape
    part = tree_sum([keep, swap(send, "seq", 1)]).reshape(4, rows // 4, cols)
    got = [swap(row_of(part, mine ^ k), "dp", k) for k in (1, 2, 3)]
    part = tree_sum([row_of(part, mine)] + got)
    for stride, radix in strides(n):
        got = [swap(part, "seq", k * stride) for k in range(1, radix)]
        part = tree_sum([part] + got)
    got = [part] + [swap(part, "dp", k) for k in (1, 2, 3)]
    part = jnp.stack(
        [
            jnp.where(mine == j, got[0], jnp.where(mine == j ^ 1, got[1], jnp.where(mine == j ^ 2, got[2], got[3])))
            for j in range(4)
        ]
    ).reshape(rows, cols)
    other = swap(part, "seq", 1)
    low = jnp.where(core == 0, part, other)
    high = jnp.where(core == 0, other, part)
    return jnp.concatenate([low, high], axis=0).astype(F32)


def per_device(
    n, tokens, mask_pos, replace_ids, token_embedding_matrix, entry_scale_vector,
    input_projection_weight, increment_coefficients, conv_w, conv_b, dt_bias, decay_rate,
    gain_out, w_out, w_head,
):
    length = tokens.shape[1]
    width = w_out.shape[1]
    nb = length // SPAN
    rows = 2 * nb * 8
    gathered = jnp.concatenate(
        [tokens.astype(F32), swap(tokens, "seq", 1).astype(F32)], axis=0
    )
    for stride, radix in strides(n):
        gathered = jnp.concatenate(
            [gathered] + [swap(gathered, "seq", k * stride) for k in range(1, radix)], axis=0
        )
    shape = jax.ShapeDtypeStruct
    weights = (
        token_embedding_matrix, entry_scale_vector[None], input_projection_weight,
        increment_coefficients.T, conv_w, conv_b, dt_bias, decay_rate, gain_out[None], w_head.T,
        tokens, mask_pos, replace_ids,
    )
    masks = mask_pos.shape[1]
    wide = -(-masks // 128) * 128
    tables = pl.pallas_call(
        tables_kernel,
        in_specs=[pl.BlockSpec(memory_space=pltpu.HBM)] * len(weights),
        scratch_shapes=[pltpu.VMEM(w.shape, w.dtype) for w in weights]
        + [pltpu.VMEM((1, wide), jnp.int32)] * 2
        + [pltpu.SemaphoreType.DMA((len(weights),))],
        out_shape=(
            pltpu.VMEM((2, 2 * CONVW, 16 * KW), BF16),
            pltpu.VMEM((2 * INNER, length), F32),
            pltpu.VMEM((2, 2, HEADS, 8), F32),
            pltpu.VMEM((2, 2, HEADS, 8), F32),
            pltpu.VMEM((INNER, 128), F32),
            pltpu.VMEM((8, width), BF16),
            pltpu.VMEM((n * nb, SPAN), F32),
        ),
        compiler_params=pltpu.CompilerParams(vmem_limit_bytes=32 << 20),
        cost_estimate=pl.CostEstimate(flops=20_000_000, bytes_accessed=3_000_000, transcendentals=10_000),
        name="tables",
    )(*[pltpu.with_memory_space_constraint(w, pltpu.HBM) for w in weights])
    slots = n + 1
    spots = n - 1 if n <= 16 else 1
    operands = (gathered, *tables, w_out)
    layer_out, send, keep = pl.pallas_call(
        functools.partial(layer_kernel, n, length, lax.axis_size("dp") * masks),
        out_shape=(
            shape((length, width), BF16),
            pltpu.VMEM((INNER // 2, width), BF16),
            pltpu.VMEM((INNER // 2, width), BF16),
        ),
        out_specs=(
            pl.BlockSpec(memory_space=pltpu.HBM),
            pl.BlockSpec(memory_space=pltpu.VMEM),
            pl.BlockSpec(memory_space=pltpu.VMEM),
        ),
        scratch_shapes=[
            pltpu.VMEM((length, width), BF16),
            pltpu.SemaphoreType.DMA,
            pltpu.VMEM((n + 2, length), F32),
            pltpu.VMEM((slots, rows, SPAN), F32),
            pltpu.VMEM((slots, rows, SPAN), F32),
            pltpu.VMEM((slots, rows, SPAN), F32),
            pltpu.VMEM((slots, rows, SPAN), F32),
            pltpu.VMEM((2, INNER, 2 * length), BF16),
            pltpu.VMEM((2, 2, INNER, length), F32),
            pltpu.VMEM((2, 2, INNER, length), F32),
            pltpu.VMEM((2, INNER, spots * length), BF16),
            pltpu.VMEM((2, 2 * STATE, spots * length), BF16),
            pltpu.VMEM((2, INNER, 2 * STATE), F32),
            pltpu.VMEM((2, INNER, length), F32),
            pltpu.VMEM((INNER, length), BF16),
        ],
        compiler_params=pltpu.CompilerParams(vmem_limit_bytes=32 << 20),
        cost_estimate=pl.CostEstimate(flops=2_000_000_000, bytes_accessed=4_000_000, transcendentals=4_000_000),
        name="layer",
    )(*operands)
    return (layer_out[None], sum_all(send, keep, n))


def solution(mesh):
    in_specs = (P("dp", "seq"), P("dp", None), P("dp", None)) + (P(),) * 11
    out_specs = (P("dp", "seq", None), P())
    return jax.shard_map(
        functools.partial(per_device, mesh.shape["seq"]),
        mesh=mesh, in_specs=in_specs, out_specs=out_specs, check_vma=False,
    )
```
